256 devices in a mesh: dp: 64 (over y, z, core), fsdp: 4 (over x).
Axes of the slice: x: 4, y: 4, z: 8, core: 2. Of those that a mesh axis runs over, the one named last changes fastest.
Arguments:
- tokens: bfloat16 [65536, 5120], P(('dp', 'fsdp')), may hold values from -6 to 6
- cotangent: bfloat16 [65536, 1024], P(('dp', 'fsdp')), may hold values from -6 to 6
- tenant: int32 [65536, 1], P(('dp', 'fsdp')), may hold values from 0 to 63; in each aligned block of 256 rows (0 to 255, 256 to 511, ...) at most 8 rows name the same one
- adapter_per_slot: int32 [64], replicated, may hold values from 0 to 63, each once
- frozen_value_weight: bfloat16 [5120, 1024], P('fsdp'), may hold values from -0.078125 to 0.078125
- down_factors: float32 [64, 5120, 64], P('dp', 'fsdp'), may hold values from -0.078125 to 0.078125
- up_factors: float32 [64, 64, 1024], P('dp', None, 'fsdp'), may hold values from -0.75 to 0.75
- down_first_moment: float32 [64, 5120, 64], P('dp', 'fsdp'), may hold values from -60 to 60
- down_second_moment: float32 [64, 5120, 64], P('dp', 'fsdp'), may hold values from 100 to 2000
- up_first_moment: float32 [64, 64, 1024], P('dp', None, 'fsdp'), may hold values from -18 to 18
- up_second_moment: float32 [64, 64, 1024], P('dp', None, 'fsdp'), may hold values from 10 to 200
Outputs:
- output: bfloat16 [65536, 1024], P(('dp', 'fsdp'))
- token_gradient: bfloat16 [65536, 5120], P(('dp', 'fsdp'))
- next_down_factors: float32 [64, 5120, 64], P('dp', 'fsdp')
- next_up_factors: float32 [64, 64, 1024], P('dp', None, 'fsdp')
- next_down_first: float32 [64, 5120, 64], P('dp', 'fsdp')
- next_down_second: float32 [64, 5120, 64], P('dp', 'fsdp')
- next_up_first: float32 [64, 64, 1024], P('dp', None, 'fsdp')
- next_up_second: float32 [64, 64, 1024], P('dp', None, 'fsdp')
The draws below stay inside these ranges and needn't reach their ends.
Inputs may be any that keep to these rules, and one draw needn't show every extreme that they name: `tenant`: in the rows of one device no adapter is named more than 8 times; in every draw some device names one adapter exactly 8 times. `adapter_per_slot`: each adapter appears exactly once.
All inputs are finite; a program needn't handle non-finite values.
Results may differ from the reference program's by a relative error of at most 0.006.
Values may be sent and summed in bfloat16 or wider, within the bound.
No kernel may reach another device: no remote copies, remote signals or barrier semaphores. Data moves between devices by JAX's collectives and lax.ppermute only.
A program may use at most 128 MiB of HBM per device.

```python
import math
import jax
import jax.numpy as jnp
import numpy as np
from jax import lax

MODEL_WIDTH = 5120
KEY_VALUE_WIDTH = 1024
ADAPTER_RANK = 64
TOK_DEV = 256
TOKENS = 65536
ADAPTER_COUNT = 64
CAP = 8
N_DP = 64
N_FSDP = 4


def steps_of(rng, extent, shards, least, high):
    factor_of, own = 1.0, jax.random.fold_in(rng, 6)
    for dim, blocks in shards:
        draws = jnp.exp(jax.random.uniform(jax.random.fold_in(own, dim), (blocks,), jnp.float32, least / len(shards), high / len(shards)))
        factor_of = factor_of * jnp.repeat(draws, extent[dim] // blocks).reshape([-1 if axis == dim else 1 for axis in range(len(extent))])
    return factor_of


def routed_block(rng, own, number, rows, amount, top, most, skew):
    ranking = jax.random.permutation(rng, amount)
    packed, usual = portions_of(amount, rows * top, most, skew, True), portions_of(amount, rows * top, most, skew, False)
    places = jnp.arange(amount)

    def named(sizes, turn):
        used = int((sizes > 0).sum())
        fixed = max(1, used // 4)
        passed = fixed + (places - fixed + turn * (used - fixed)) % max(1, amount - fixed)
        return jnp.zeros((amount,), jnp.int32).at[ranking[jnp.where(places < fixed, places, passed)]].set(jnp.asarray(sizes, jnp.int32))

    sizes = jnp.where(number % 4 == 0, named(packed, number // 4), named(usual, number - number // 4 - 1))
    mixed = jax.random.permutation(jax.random.fold_in(own, 3), amount)
    source_of, receiver = mixed[0:amount // 2 * 2:2], mixed[1:amount // 2 * 2:2]
    room = jnp.minimum(sizes[source_of] - 1, most - sizes[receiver]) // 2
    room = jnp.where((source_of == ranking[0]) | (receiver == ranking[0]) | (sizes[receiver] == 0), 0, jnp.maximum(room, 0))
    passed = jax.random.randint(jax.random.fold_in(own, 4), (amount // 2,), 0, 1 << 20) % (room + 1)
    sizes = sizes.at[source_of].add(-passed).at[receiver].add(passed)
    items = jnp.searchsorted(jnp.cumsum(sizes), jnp.arange(rows * top), side="right").astype(jnp.int32)
    listing = items.reshape(top, rows).T
    listing = listing[jax.random.permutation(jax.random.fold_in(own, 1), rows)]
    turn = jax.random.randint(jax.random.fold_in(own, 2), (rows, 1), 0, top)
    return jnp.take_along_axis(listing, (jnp.arange(top)[None, :] + turn) % top, axis=1)


def portions_of(amount, total, bound, lean, full):
    portions = [(1 << 20) // math.isqrt(rank ** lean) + 1 for rank in range(1, amount + 1)]
    largest = bound if full else min(bound, max(-(-total // amount), total * portions[0] // sum(portions)))
    least = 1 if total - largest >= amount - 1 else 0
    holding, spare = [largest] + [least] * (amount - 1), total - largest - least * (amount - 1)
    while spare > 0:
        movable = [i for i in range(1, amount) if holding[i] < largest] or [i for i in range(1, amount) if holding[i] < bound]
        pool, budget = sum([portions[i] for i in movable]), spare
        for i in movable:
            extra = min(bound - holding[i], max(1, budget * portions[i] // pool), spare)
            holding[i] = holding[i] + extra
            spare = spare - extra
    return np.array(holding)


def noise(key, extent, spread, limit, pieces=(), kind=jnp.bfloat16):
    values = spread * jax.random.normal(key, extent, jnp.float32)
    if pieces:
        values = values * steps_of(key, extent, pieces, -0.22, 0.18)
    return jnp.clip(values, -limit, limit).astype(kind)


def setup_inputs(seed: int = 0) -> dict:
    streams_of = jax.random.split(jax.random.key(seed), 12)
    tokens = noise(streams_of[0], (TOKENS, MODEL_WIDTH), 1.0, 6.0, ((0, 256),))
    cotangent = noise(streams_of[1], (TOKENS, KEY_VALUE_WIDTH), 1.0, 6.0, ((0, 256),))
    tenant_keys = jax.random.split(jax.random.fold_in(streams_of[2], 1), TOKENS // TOK_DEV)
    tenant_turns = jax.random.permutation(jax.random.fold_in(streams_of[2], 3), TOKENS // TOK_DEV)
    tenant = jax.vmap(lambda own, number: routed_block(jax.random.fold_in(streams_of[2], 2), own, number, TOK_DEV, ADAPTER_COUNT, 1, CAP, 2))(tenant_keys, tenant_turns).reshape((TOKENS, 1))
    adapter_per_slot = jax.random.permutation(streams_of[3], ADAPTER_COUNT).astype(jnp.int32)
    frozen_value_weight = noise(streams_of[4], (MODEL_WIDTH, KEY_VALUE_WIDTH), MODEL_WIDTH ** -0.5, 0.078125, ((0, 4),))
    down_factors = noise(streams_of[5], (ADAPTER_COUNT, MODEL_WIDTH, ADAPTER_RANK), MODEL_WIDTH ** -0.5, 0.078125, ((0, 64), (1, 4)), jnp.float32)
    up_factors = noise(streams_of[6], (ADAPTER_COUNT, ADAPTER_RANK, KEY_VALUE_WIDTH), ADAPTER_RANK ** -0.5, 0.75, ((0, 64), (2, 4)), jnp.float32)
    down_first_moment = noise(streams_of[7], (ADAPTER_COUNT, MODEL_WIDTH, ADAPTER_RANK), 10.0, 60.0, ((0, 64), (1, 4)), jnp.float32)
    down_second_moment = jnp.clip(jnp.exp(math.log(2000.0) - 2.9957323 * jax.random.uniform(streams_of[8], (ADAPTER_COUNT, MODEL_WIDTH, ADAPTER_RANK), jnp.float32) ** steps_of(streams_of[8], (ADAPTER_COUNT, MODEL_WIDTH, ADAPTER_RANK), ((0, 64), (1, 4)), -0.2, 0.2)), 100.0, 2000.0)
    up_first_moment = noise(streams_of[9], (ADAPTER_COUNT, ADAPTER_RANK, KEY_VALUE_WIDTH), 3.0, 18.0, ((0, 64), (2, 4)), jnp.float32)
    up_second_moment = jnp.clip(jnp.exp(math.log(200.0) - 2.9957323 * jax.random.uniform(streams_of[10], (ADAPTER_COUNT, ADAPTER_RANK, KEY_VALUE_WIDTH), jnp.float32) ** steps_of(streams_of[10], (ADAPTER_COUNT, ADAPTER_RANK, KEY_VALUE_WIDTH), ((0, 64), (2, 4)), -0.2, 0.2)), 10.0, 200.0)
    return {"tokens": tokens, "cotangent": cotangent, "tenant": tenant, "adapter_per_slot": adapter_per_slot, "frozen_value_weight": frozen_value_weight, "down_factors": down_factors, "up_factors": up_factors, "down_first_moment": down_first_moment, "down_second_moment": down_second_moment, "up_first_moment": up_first_moment, "up_second_moment": up_second_moment}


ADAPTER_SCALE = 0.25
BETA_ONE = 0.9
BETA_TWO = 0.99
ADAM_STEP = 10.0
ADAM_RATE = 0.02
ADAM_EPS = 1e-08

def moment_update(master, first_moment, second_moment, gradient):
    first_new = BETA_ONE * first_moment + (1.0 - BETA_ONE) * gradient
    second_new = BETA_TWO * second_moment + (1.0 - BETA_TWO) * gradient * gradient
    first_hat = first_new / (1.0 - BETA_ONE ** ADAM_STEP)
    second_hat = second_new / (1.0 - BETA_TWO ** ADAM_STEP)
    updated = master - ADAM_RATE * first_hat / (jnp.sqrt(second_hat) + ADAM_EPS)
    return (updated, first_new, second_new)

def reference(tokens, cotangent, tenant, adapter_per_slot, frozen_value_weight, down_factors, up_factors, down_first_moment, down_second_moment, up_first_moment, up_second_moment):
    row_total = tokens.shape[0]
    adapter_ids = tenant[:, 0].astype(jnp.int32)
    count_table = lax.optimization_barrier(jnp.sum((adapter_ids[:, None] == jnp.arange(ADAPTER_COUNT, dtype=jnp.int32)[None, :]).astype(jnp.int32), axis=0))
    order = jnp.argsort(adapter_ids, stable=True).astype(jnp.int32)
    offsets = (jnp.cumsum(count_table) - count_table).astype(jnp.int32)
    most_rows = N_DP * N_FSDP * CAP
    base_out = jnp.dot(tokens, frozen_value_weight, preferred_element_type=jnp.float32)
    base_in = lax.dot_general(cotangent, frozen_value_weight, (((1,), (1,)), ((), ())), preferred_element_type=jnp.float32)

    def slot_step(carry, slot_number):
        output_total, input_total = carry
        adapter = adapter_per_slot[slot_number]
        positions = jnp.arange(most_rows, dtype=jnp.int32)
        active_mask = positions < count_table[adapter]
        selected_rows = order[jnp.minimum(offsets[adapter] + positions, row_total - 1)].astype(jnp.int32)
        input_rows = jnp.where(active_mask[:, None], tokens[selected_rows], jnp.zeros((), tokens.dtype))
        output_grad_rows = jnp.where(active_mask[:, None], cotangent[selected_rows], jnp.zeros((), cotangent.dtype))
        down_matrix = down_factors[slot_number].astype(jnp.bfloat16)
        up_matrix = up_factors[slot_number].astype(jnp.bfloat16)
        reduced_rows = (ADAPTER_SCALE * jnp.dot(input_rows, down_matrix, preferred_element_type=jnp.float32)).astype(jnp.bfloat16)
        adapter_output = jnp.dot(reduced_rows, up_matrix, preferred_element_type=jnp.float32).astype(jnp.bfloat16)
        reduced_gradient = (ADAPTER_SCALE * lax.dot_general(output_grad_rows, up_matrix, (((1,), (1,)), ((), ())), preferred_element_type=jnp.float32)).astype(jnp.bfloat16)
        adapter_input = lax.dot_general(reduced_gradient, down_matrix, (((1,), (1,)), ((), ())), preferred_element_type=jnp.float32).astype(jnp.bfloat16)
        grad_a = lax.dot_general(input_rows, reduced_gradient, (((0,), (0,)), ((), ())), preferred_element_type=jnp.float32)
        grad_b = lax.dot_general(reduced_rows, output_grad_rows, (((0,), (0,)), ((), ())), preferred_element_type=jnp.float32)
        empty_output = jnp.zeros(adapter_output.shape, jnp.float32)
        empty_input = jnp.zeros(adapter_input.shape, jnp.float32)
        output_total = output_total.at[selected_rows].add(jnp.where(active_mask[:, None], adapter_output.astype(jnp.float32), empty_output))
        input_total = input_total.at[selected_rows].add(jnp.where(active_mask[:, None], adapter_input.astype(jnp.float32), empty_input))
        return ((output_total, input_total), (grad_a, grad_b))
    (output_total, input_total), (down_gradients, up_gradients) = lax.scan(slot_step, (base_out, base_in), jnp.arange(ADAPTER_COUNT, dtype=jnp.int32))
    output = output_total.astype(jnp.bfloat16)
    token_gradient = input_total.astype(jnp.bfloat16)
    next_down_factors, next_down_first, next_down_second = moment_update(down_factors, down_first_moment, down_second_moment, down_gradients)
    next_up_factors, next_up_first, next_up_second = moment_update(up_factors, up_first_moment, up_second_moment, up_gradients)
    return (output, token_gradient, next_down_factors, next_up_factors, next_down_first, next_down_second, next_up_first, next_up_second)
```

```python
import jax
import jax.numpy as jnp
from jax import lax
from jax.experimental import pallas as pl
from jax.experimental.pallas import tpu as pltpu
from jax.sharding import Mesh, PartitionSpec as P

ADAPTER_SCALE = 0.25
BETA_ONE = 0.9
BETA_TWO = 0.99
ADAM_STEP = 10.0
ADAM_RATE = 0.02
ADAM_EPS = 1e-08

NY, NZ, NC, NX = 4, 8, 2, 4
ROWS = 256
MODEL = 5120
KV = 1024
RANK = 64
MS = MODEL // NX
KS = KV // NX
WIDE = MS + KS
HALF = WIDE // 2
REST = MS - HALF
CAP = 8
GROUP_ROWS = NY * CAP
SLOTS = NZ * GROUP_ROWS
COLS = NY * RANK
BF = jnp.bfloat16
F32 = jnp.float32
VMEM_BYTES = 56 * 1024 * 1024


def shift(count, step):
    return [(i, (i + step) % count) for i in range(count)]


def along_x(array, step):
    return lax.ppermute(array, "x", shift(NX, step))


def along_y(array, step):
    return lax.ppermute(array, "y", shift(NY, step))


def along_z(array, step):
    return lax.ppermute(array, "z", shift(NZ, step))


def other_core(array):
    return lax.ppermute(array, "c", shift(NC, 1))


def moment_update(master, first_moment, second_moment, gradient):
    first_new = BETA_ONE * first_moment + (1.0 - BETA_ONE) * gradient
    second_new = BETA_TWO * second_moment + (1.0 - BETA_TWO) * gradient * gradient
    first_hat = first_new / (1.0 - BETA_ONE**ADAM_STEP)
    second_hat = second_new / (1.0 - BETA_TWO**ADAM_STEP)
    updated = master - ADAM_RATE * first_hat / (jnp.sqrt(second_hat) + ADAM_EPS)
    return (updated, first_new, second_new)


def dot(a, b):
    return jnp.dot(a, b, preferred_element_type=F32)


def dot_t(a, b):
    return lax.dot_general(a, b, (((1,), (1,)), ((), ())), preferred_element_type=F32)


def dot_tn(a, b):
    return lax.dot_general(a, b, (((0,), (0,)), ((), ())), preferred_element_type=F32)


def gather_weights(wide):
    left, right = wide[:, :HALF], wide[:, HALF:]
    by_y = jnp.stack([right] + [along_y(right, k) for k in range(1, NY)]).reshape(COLS, HALF)
    by_z = [None] * NZ
    by_z[0] = up = down = left
    for k in range(1, NZ // 2 + 1):
        up = by_z[k] = along_z(up, 1)
        if k < NZ // 2:
            down = by_z[NZ - k] = along_z(down, -1)
    by_z = jnp.stack(by_z)
    whole_right = [None] * NZ
    whole_right[0] = up = down = by_y
    one, three = along_y(by_z, 1), along_y(by_z, -1)
    two = [along_y(one[: NZ // 2], 1), along_y(three[NZ // 2 :], -1)]
    for k in range(1, NZ // 2 + 1):
        up = whole_right[k] = along_z(up, 1)
        if k < NZ // 2:
            down = whole_right[NZ - k] = along_z(down, -1)
    whole_left = jnp.stack([by_z, one, jnp.concatenate(two), three])
    return whole_left, jnp.stack(whole_right)


def add(a, b):
    return (a.astype(F32) + b.astype(F32)).astype(BF)


def scatter_gradients(left, right):
    half = NZ // 2
    a, b = along_y(left[2][:half], -1), along_y(left[2][half:], 1)
    up, down = along_z(right[5], 1), along_z(right[4], -1)
    one = along_y(jnp.concatenate([add(left[1][:half], a), left[1][half:]]), -1)
    three = along_y(jnp.concatenate([left[3][:half], add(left[3][half:], b)]), 1)
    for k in range(1, 4):
        down = along_z(add(down, right[4 - k]), -1)
        if k < 3:
            up = along_z(add(up, right[5 + k]), 1)
    right = add(add(right[0], down), up).reshape(NY, RANK, HALF)
    left = add(add(left[0], one), three)
    up, down = along_z(left[5], 1), along_z(left[4], -1)
    near = [along_y(right[k], -k) for k in range(1, NY)]
    for k in range(1, 4):
        down = along_z(add(down, left[4 - k]), -1)
        if k < 3:
            up = along_z(add(up, left[5 + k]), 1)
    left = left[0].astype(F32) + down + up
    right = right[0].astype(F32) + near[0] + near[1] + near[2]
    return jnp.concatenate([left, right], axis=1)


def params():
    return pltpu.CompilerParams(vmem_limit_bytes=VMEM_BYTES)


def one_hot(codes):
    slots = lax.broadcasted_iota(jnp.int32, (SLOTS, ROWS), 0)
    return (slots == codes).astype(BF)


def spread_kernel(codes, r0, r1, r2, r3, out):
    for k, rows in enumerate((r0, r1, r2, r3)):
        placed = dot(one_hot(codes[k]), rows[...]).astype(BF)
        out[:, k] = placed.reshape(NZ, GROUP_ROWS, WIDE)


def spread(codes, pieces):
    return pl.pallas_call(
        spread_kernel,
        out_shape=jax.ShapeDtypeStruct((NZ, NX, GROUP_ROWS, WIDE), BF),
        compiler_params=params(),
        name="spread_rows",
    )(codes, *pieces)


def row_mask():
    rows = lax.broadcasted_iota(jnp.int32, (2 * NX * GROUP_ROWS, COLS), 0)
    cols = lax.broadcasted_iota(jnp.int32, (2 * NX * GROUP_ROWS, COLS), 1)
    return lax.rem(rows, GROUP_ROWS) // CAP == cols // RANK


def fold(product, mask):
    kept = jnp.where(mask, product, 0.0)
    half = kept[:, : 2 * RANK] + kept[:, 2 * RANK :]
    return half + pltpu.roll(half, RANK, 1)


def low_kernel(own, oth, left, right, out):
    mask = row_mask()
    rows = 2 * NX * GROUP_ROWS
    s = jnp.concatenate(
        [own[...].reshape(rows // 2, WIDE), oth[...].reshape(rows // 2, WIDE)], axis=0
    )
    wl = left[...].reshape(COLS, HALF)
    wr = right[...].reshape(COLS, HALF)
    low = dot_t(s[:, :HALF], wl) + dot_t(s[:, HALF:MS], wr[:, :REST])
    grad = dot_t(s[:, MS:], wr[:, REST:])
    lanes = lax.broadcasted_iota(jnp.int32, (rows, 2 * RANK), 1)
    out[0] = jnp.where(lanes < RANK, fold(low, mask), fold(grad, mask)).astype(BF)


def slot_spec():
    return pl.BlockSpec((1, NX, GROUP_ROWS, WIDE), lambda g: (g, 0, 0, 0))


def left_spec():
    return pl.BlockSpec((NY, 1, RANK, HALF), lambda g: (0, g, 0, 0))


def right_spec():
    return pl.BlockSpec((1, COLS, HALF), lambda g: (g, 0, 0))


def low_spec():
    return pl.BlockSpec((1, 2 * NX * GROUP_ROWS, 2 * RANK), lambda g: (g, 0, 0))


def low_partial(own, oth, left, right):
    return pl.pallas_call(
        low_kernel,
        grid=(NZ,),
        in_specs=[slot_spec(), slot_spec(), left_spec(), right_spec()],
        out_specs=low_spec(),
        out_shape=jax.ShapeDtypeStruct((NZ, 2 * NX * GROUP_ROWS, 2 * RANK), BF),
        compiler_params=params(),
        name="low_partial",
    )(own, oth, left, right)


def sum_over_x(partial, me):
    share = NZ // NX
    parts = [
        lax.dynamic_slice_in_dim(partial, share * ((me + k) % NX), share, 0) for k in range(NX)
    ]

    def from_left(array, k):
        by_source = along_x(array, k).reshape(share, NC, NX, GROUP_ROWS, 2 * RANK)
        return jnp.roll(by_source, k, axis=2).reshape(array.shape)

    total = parts[0].astype(F32)
    for k in range(1, NX):
        total = total + from_left(parts[k], k).astype(F32)
    mine = (ADAPTER_SCALE * total).astype(BF)
    back = [from_left(mine, 3), from_left(mine, 2), from_left(mine, 1), mine]
    return lax.dynamic_slice_in_dim(jnp.concatenate(back + back), share * (NX - 1 - me), NZ, 0)


def adapter_kernel(low, own, oth, left, right, own_out, oth_out, grad_left, grad_right):
    mask = row_mask()
    rows = 2 * NX * GROUP_ROWS
    s = jnp.concatenate(
        [own[...].reshape(rows // 2, WIDE), oth[...].reshape(rows // 2, WIDE)], axis=0
    )
    wl = left[...].reshape(COLS, HALF)
    wr = right[...].reshape(COLS, HALF)
    both = low[0].astype(F32)
    turned = pltpu.roll(both, RANK, 1)
    lanes = lax.broadcasted_iota(jnp.int32, both.shape, 1)
    reduced = jnp.where(lanes < RANK, both, turned)
    gradient = jnp.where(lanes < RANK, turned, both)
    reduced = jnp.where(mask, jnp.concatenate([reduced, reduced], axis=1), 0.0).astype(BF)
    gradient = jnp.where(mask, jnp.concatenate([gradient, gradient], axis=1), 0.0).astype(BF)
    terms = jnp.concatenate(
        [
            dot(gradient, wl).astype(BF),
            dot(gradient, wr[:, :REST]).astype(BF),
            dot(reduced, wr[:, REST:]).astype(BF),
        ],
        axis=1,
    )
    own_out[...] = terms[: rows // 2].reshape(own_out.shape)
    oth_out[...] = terms[rows // 2 :].reshape(oth_out.shape)
    grad_left[...] = dot_tn(gradient, s[:, :HALF]).astype(BF).reshape(grad_left.shape)
    grad_right[0, :, :REST] = dot_tn(gradient, s[:, HALF:MS]).astype(BF)
    grad_right[0, :, REST:] = dot_tn(reduced, s[:, MS:]).astype(BF)


def adapter_terms(low, own, oth, left, right):
    return pl.pallas_call(
        adapter_kernel,
        grid=(NZ,),
        in_specs=[low_spec(), slot_spec(), slot_spec(), left_spec(), right_spec()],
        out_specs=[slot_spec(), slot_spec(), left_spec(), right_spec()],
        out_shape=[
            jax.ShapeDtypeStruct((NZ, NX, GROUP_ROWS, WIDE), BF),
            jax.ShapeDtypeStruct((NZ, NX, GROUP_ROWS, WIDE), BF),
            jax.ShapeDtypeStruct((NY, NZ, RANK, HALF), BF),
            jax.ShapeDtypeStruct((NZ, COLS, HALF), BF),
        ],
        compiler_params=params(),
        name="adapter_terms",
    )(low, own, oth, left, right)


def collect_kernel(codes, terms, o0, o1, o2, o3):
    for k, out in enumerate((o0, o1, o2, o3)):
        placed = terms[:, k].reshape(SLOTS, WIDE)
        out[...] = dot_tn(one_hot(codes[k]), placed).astype(BF)


def collect(codes, terms):
    return pl.pallas_call(
        collect_kernel,
        out_shape=[jax.ShapeDtypeStruct((ROWS, WIDE), BF)] * NX,
        compiler_params=params(),
        name="collect_rows",
    )(codes, terms)


def finish_kernel(codes, terms, n0, n1, n2, n3, d0, d1, d2, d3, weight, o0, o1, o2, o3):
    w = weight[...]
    groups = zip((n0, n1, n2, n3), (d0, d1, d2, d3), (o0, o1, o2, o3), strict=True)
    for k, (other, cot, out) in enumerate(groups):
        placed = terms[:, k].reshape(SLOTS, WIDE)
        rows = dot_tn(one_hot(codes[k]), placed) + other[...].astype(F32)
        out[:, :MS] = (rows[:, :MS] + dot_t(cot[...], w)).astype(BF)
        out[:, MS:] = rows[:, MS:].astype(BF)


def finish(codes, terms, others, cots, weight):
    return pl.pallas_call(
        finish_kernel,
        out_shape=[jax.ShapeDtypeStruct((ROWS, WIDE), BF)] * NX,
        compiler_params=params(),
        name="token_gradient",
    )(codes, terms, *others, *cots, weight)


def local(
    tokens,
    cotangent,
    tenant,
    adapter_per_slot,
    frozen_value_weight,
    down_factors,
    up_factors,
    down_first_moment,
    down_second_moment,
    up_first_moment,
    up_second_moment,
):
    x, y, z, c = (lax.axis_index(name) for name in ("x", "y", "z", "c"))

    wide = jnp.concatenate([down_factors[0].astype(BF).T, up_factors[0].astype(BF)], axis=1)

    matches = (tenant == adapter_per_slot[None, :]).astype(jnp.int32)
    earlier = jnp.cumsum(matches, axis=0) - matches
    place = jnp.sum(matches * earlier, axis=1)
    owner = jnp.sum(matches * jnp.arange(NY * NZ * NC, dtype=jnp.int32)[None, :], axis=1)
    far_y = (y - owner // (NZ * NC)) % NY
    far_z = (z - owner // NC % NZ) % NZ
    code = ((owner % NC) * SLOTS + far_z * GROUP_ROWS + far_y * CAP + place).reshape(1, ROWS)
    codes = jnp.stack([code] + [along_x(code, k) for k in range(1, NX)])
    codes_oth = other_core(codes) - c * SLOTS
    codes_own = codes - c * SLOTS

    def piece(k):
        to = (x + k) % NX
        return jnp.concatenate(
            [
                lax.dynamic_slice_in_dim(tokens, to * MS, MS, 1),
                lax.dynamic_slice_in_dim(cotangent, to * KS, KS, 1),
            ],
            axis=1,
        )

    pieces = [piece(0)] + [along_x(piece(k), k) for k in range(1, NX)]
    pieces_oth = [other_core(p) for p in pieces]
    left, right = gather_weights(wide)
    cots = [cotangent] + [along_x(cotangent, k) for k in range(1, NX)]

    own = spread(codes_own, pieces)
    oth = spread(codes_oth, pieces_oth)
    low = sum_over_x(low_partial(own, oth, left, right), x)
    base = [dot(p[:, :MS], frozen_value_weight) for p in pieces]
    base = [base[0]] + [along_x(base[k].astype(BF), -k).astype(F32) for k in range(1, NX)]

    own_terms, oth_terms, grad_left, grad_right = adapter_terms(low, own, oth, left, right)
    others = [other_core(t) for t in collect(codes_oth, oth_terms)]
    done = finish(codes_own, own_terms, others, cots, frozen_value_weight)
    done = [done[0]] + [along_x(done[k], -k) for k in range(1, NX)]
    gradient = scatter_gradients(grad_left, grad_right)

    token_gradient = jnp.zeros((ROWS, MODEL), BF)
    lora_out = jnp.zeros((ROWS, KV), BF)
    for k in range(NX):
        at = (x + k) % NX
        token_gradient = lax.dynamic_update_slice_in_dim(
            token_gradient, done[k][:, :MS], at * MS, 1
        )
        lora_out = lax.dynamic_update_slice_in_dim(lora_out, done[k][:, MS:], at * KS, 1)
    output = (base[0] + base[1] + base[2] + base[3] + lora_out.astype(F32)).astype(BF)

    next_down_factors, next_down_first, next_down_second = moment_update(
        down_factors, down_first_moment, down_second_moment, gradient[:, :MS].T[None]
    )
    next_up_factors, next_up_first, next_up_second = moment_update(
        up_factors, up_first_moment, up_second_moment, gradient[:, MS:][None]
    )
    return (
        output,
        token_gradient,
        next_down_factors,
        next_up_factors,
        next_down_first,
        next_down_second,
        next_up_first,
        next_up_second,
    )


def solution(mesh):
    fine = Mesh(mesh.devices.reshape(NY, NZ, NC, NX), ("y", "z", "c", "x"))
    dp = ("y", "z", "c")
    rows = P((*dp, "x"), None)
    down = P(dp, "x", None)
    up = P(dp, None, "x")
    return jax.shard_map(
        local,
        mesh=fine,
        in_specs=(rows, rows, rows, P(), P("x", None), down, up, down, down, up, up),
        out_specs=(rows, rows, down, up, down, down, up, up),
        check_vma=False,
    )
```

```python
import jax
import jax.numpy as jnp
from jax import lax
from jax.experimental import pallas as pl
from jax.experimental.pallas import tpu as pltpu
from jax.sharding import Mesh, PartitionSpec as P

ADAPTER_SCALE = 0.25
BETA_ONE = 0.9
BETA_TWO = 0.99
ADAM_STEP = 10.0
ADAM_RATE = 0.02
ADAM_EPS = 1e-08

NY, NZ, NC, NX = 4, 8, 2, 4
ROWS = 256
MODEL = 5120
KV = 1024
RANK = 64
MS = MODEL // NX
KS = KV // NX
WIDE = MS + KS
LEFT = 640
RIGHT = WIDE - LEFT
REST = MS - LEFT
BOTH = MS + KV
CAP = 8
GROUP_ROWS = NY * CAP
SLOTS = NZ * GROUP_ROWS
COLS = NY * RANK
BF = jnp.bfloat16
F32 = jnp.float32


def exchange(array, axis):
    return lax.all_to_all(array, axis, split_axis=0, concat_axis=0, tiled=True)


def gather(array, axis, count):
    return exchange(jnp.broadcast_to(array[None], (count, *array.shape)), axis)


def total(array):
    return jnp.sum(array.astype(F32), axis=0)


def shift(count, step):
    return [(i, (i + step) % count) for i in range(count)]


def along_y(array, step):
    return lax.ppermute(array, "y", shift(NY, step))


def along_z(array, step):
    return lax.ppermute(array, "z", shift(NZ, step))


def other_core(array):
    return lax.ppermute(array, "c", shift(NC, 1))


def moment_update(master, first_moment, second_moment, gradient):
    first_new = BETA_ONE * first_moment + (1.0 - BETA_ONE) * gradient
    second_new = BETA_TWO * second_moment + (1.0 - BETA_TWO) * gradient * gradient
    first_hat = first_new / (1.0 - BETA_ONE**ADAM_STEP)
    second_hat = second_new / (1.0 - BETA_TWO**ADAM_STEP)
    updated = master - ADAM_RATE * first_hat / (jnp.sqrt(second_hat) + ADAM_EPS)
    return (updated, first_new, second_new)


def dot(a, b):
    return jnp.dot(a, b, preferred_element_type=F32)


def dot_t(a, b):
    return lax.dot_general(a, b, (((1,), (1,)), ((), ())), preferred_element_type=F32)


def dot_tn(a, b):
    return lax.dot_general(a, b, (((0,), (0,)), ((), ())), preferred_element_type=F32)


def gather_weights(wide, z, rows):
    left, right = wide[:, :LEFT], wide[:, LEFT:]
    half = NZ // 2
    left = lax.all_gather(left, "z", axis=0)
    right = jnp.stack([right] + [along_y(right, k) for k in range(1, NY)]).reshape(1, COLS, RIGHT)
    right, rows = lax.optimization_barrier((right, rows))
    rows = exchange(rows, "x")
    whole = jnp.zeros((NZ, COLS, RIGHT), BF)
    whole = lax.dynamic_update_slice_in_dim(whole, right, z, 0)
    up = down = right
    one, three = along_y(left, 1), along_y(left, -1)
    for k in range(1, half + 1):
        up = along_z(up, 1)
        whole = lax.dynamic_update_slice_in_dim(whole, up, (z - k) % NZ, 0)
        if k < half:
            down = along_z(down, -1)
            whole = lax.dynamic_update_slice_in_dim(whole, down, (z + k) % NZ, 0)
        if k == half - 1:
            up, down, rows, one, three = lax.optimization_barrier((up, down, rows, one, three))
    two = [along_y(one[:half], 1), along_y(three[half:], -1)]
    return jnp.stack([left, one, jnp.concatenate(two), three]), whole, rows


def add(a, b):
    return (a.astype(F32) + b.astype(F32)).astype(BF)


def scatter_gradients(left, right, z, after, first):
    half = NZ // 2

    def part(k):
        return lax.dynamic_index_in_dim(right, (z + k) % NZ, 0, keepdims=False)

    a, b = along_y(left[2][:half], -1), along_y(left[2][half:], 1)
    down, up = along_z(part(-4), -1), along_z(part(3), 1)
    one = along_y(jnp.concatenate([add(left[1][:half], a), left[1][half:]]), -1)
    three = along_y(jnp.concatenate([left[3][:half], add(left[3][half:], b)]), 1)
    down, up = along_z(add(down, part(-3)), -1), along_z(add(up, part(2)), 1)
    down, up, one, three, _ = lax.optimization_barrier((down, up, one, three, after))
    left = (left[0].astype(F32) + one + three).astype(BF)
    left = lax.psum_scatter(left, "z", scatter_dimension=0, tiled=False)
    down, up = along_z(add(down, part(-2)), -1), along_z(add(up, part(1)), 1)
    down, up, first = lax.optimization_barrier((down, up, first))
    down = along_z(add(down, part(-1)), -1)
    right = (part(0).astype(F32) + down + up).astype(BF).reshape(NY, RANK, RIGHT)
    near = [along_y(right[k], -k) for k in range(1, NY)]
    right = right[0].astype(F32) + near[0] + near[1] + near[2]
    return jnp.concatenate([left.astype(F32), right], axis=1), first


def params(megabytes=20):
    return pltpu.CompilerParams(vmem_limit_bytes=megabytes * 1024 * 1024)


def one_hot(codes):
    slots = lax.broadcasted_iota(jnp.int32, (NC * SLOTS, ROWS), 0)
    return (slots == codes).astype(BF)


def spread_kernel(x, codes, rows, cot, own, oth):
    place = one_hot(codes[0])
    for at, part in ((0, rows[0, :, :MS]), (MS, cot[0])):
        width = part.shape[1]
        placed = dot(place, part).astype(BF)
        own[:, 0, :, at : at + width] = placed[:SLOTS].reshape(NZ, GROUP_ROWS, width)
        oth[:, 0, :, at : at + width] = placed[SLOTS:].reshape(NZ, GROUP_ROWS, width)


def spread(x, codes, rows):
    out = pl.BlockSpec((NZ, 1, GROUP_ROWS, WIDE), lambda i, x: (0, i, 0, 0))
    return pl.pallas_call(
        spread_kernel,
        grid_spec=pltpu.PrefetchScalarGridSpec(
            num_scalar_prefetch=1,
            grid=(NX,),
            in_specs=[
                pl.BlockSpec((1, 1, ROWS), lambda i, x: (i, 0, 0)),
                pl.BlockSpec((1, ROWS, BOTH), lambda i, x: (i, 0, 0)),
                pl.BlockSpec((1, ROWS, KS), lambda i, x: (i, 0, MS // KS + x[0])),
            ],
            out_specs=[out, out],
        ),
        out_shape=[jax.ShapeDtypeStruct((NZ, NX, GROUP_ROWS, WIDE), BF)] * 2,
        compiler_params=params(),
        name="spread_rows",
    )(x, codes, rows, rows)


def row_mask():
    rows = lax.broadcasted_iota(jnp.int32, (2 * NX * GROUP_ROWS, COLS), 0)
    cols = lax.broadcasted_iota(jnp.int32, (2 * NX * GROUP_ROWS, COLS), 1)
    return lax.rem(rows, GROUP_ROWS) // CAP == cols // RANK


def fold(product, mask):
    kept = jnp.where(mask, product, 0.0)
    half = kept[:, : 2 * RANK] + kept[:, 2 * RANK :]
    return half + pltpu.roll(half, RANK, 1)


def low_kernel(own, oth, left, right, out):
    mask = row_mask()
    rows = 2 * NX * GROUP_ROWS
    s = jnp.concatenate(
        [own[...].reshape(rows // 2, WIDE), oth[...].reshape(rows // 2, WIDE)], axis=0
    )
    wl = left[...].reshape(COLS, LEFT)
    wr = right[...].reshape(COLS, RIGHT)
    low = dot_t(s[:, :LEFT], wl) + dot_t(s[:, LEFT:MS], wr[:, :REST])
    grad = dot_t(s[:, MS:], wr[:, REST:])
    lanes = lax.broadcasted_iota(jnp.int32, (rows, 2 * RANK), 1)
    out[0] = jnp.where(lanes < RANK, fold(low, mask), fold(grad, mask)).astype(BF)


def slot_spec():
    return pl.BlockSpec((1, NX, GROUP_ROWS, WIDE), lambda g: (g, 0, 0, 0))


def left_spec():
    return pl.BlockSpec((NY, 1, RANK, LEFT), lambda g: (0, g, 0, 0))


def right_spec():
    return pl.BlockSpec((1, COLS, RIGHT), lambda g: (g, 0, 0))


def low_spec():
    return pl.BlockSpec((1, 2 * NX * GROUP_ROWS, 2 * RANK), lambda g: (g, 0, 0))


def low_partial(own, oth, left, right):
    return pl.pallas_call(
        low_kernel,
        grid=(NZ,),
        in_specs=[slot_spec(), slot_spec(), left_spec(), right_spec()],
        out_specs=low_spec(),
        out_shape=jax.ShapeDtypeStruct((NZ, 2 * NX * GROUP_ROWS, 2 * RANK), BF),
        compiler_params=params(),
        name="low_partial",
    )(own, oth, left, right)


def sum_over_x(partial):
    share = NZ // NX
    parts = exchange(partial.reshape(NX, share, *partial.shape[1:]), "x")
    mine = (ADAPTER_SCALE * total(parts)).astype(BF)
    return gather(mine, "x", NX).reshape(partial.shape)


def masked(low):
    mask = row_mask()
    both = low.astype(F32)
    turned = pltpu.roll(both, RANK, 1)
    lanes = lax.broadcasted_iota(jnp.int32, both.shape, 1)
    reduced = jnp.where(lanes < RANK, both, turned)
    gradient = jnp.where(lanes < RANK, turned, both)
    reduced = jnp.where(mask, jnp.concatenate([reduced, reduced], axis=1), 0.0).astype(BF)
    gradient = jnp.where(mask, jnp.concatenate([gradient, gradient], axis=1), 0.0).astype(BF)
    return reduced, gradient


def gradient_kernel(low, own, oth, grad_left, grad_right):
    rows = 2 * NX * GROUP_ROWS
    s = jnp.concatenate(
        [own[...].reshape(rows // 2, WIDE), oth[...].reshape(rows // 2, WIDE)], axis=0
    )
    reduced, gradient = masked(low[0])
    grad_left[...] = dot_tn(gradient, s[:, :LEFT]).astype(BF).reshape(grad_left.shape)
    grad_right[0, :, :REST] = dot_tn(gradient, s[:, LEFT:MS]).astype(BF)
    grad_right[0, :, REST:] = dot_tn(reduced, s[:, MS:]).astype(BF)


def adapter_gradients(low, own, oth):
    return pl.pallas_call(
        gradient_kernel,
        grid=(NZ,),
        in_specs=[low_spec(), slot_spec(), slot_spec()],
        out_specs=[left_spec(), right_spec()],
        out_shape=[
            jax.ShapeDtypeStruct((NY, NZ, RANK, LEFT), BF),
            jax.ShapeDtypeStruct((NZ, COLS, RIGHT), BF),
        ],
        compiler_params=params(),
        name="adapter_gradients",
    )(low, own, oth)


def term_kernel(low, left, right, own_out, oth_out):
    rows = 2 * NX * GROUP_ROWS
    wl = left[...].reshape(COLS, LEFT)
    wr = right[...].reshape(COLS, RIGHT)
    reduced, gradient = masked(low[0])
    terms = jnp.concatenate(
        [
            dot(gradient, wl).astype(BF),
            dot(gradient, wr[:, :REST]).astype(BF),
            dot(reduced, wr[:, REST:]).astype(BF),
        ],
        axis=1,
    )
    own_out[...] = terms[: rows // 2].reshape(own_out.shape)
    oth_out[...] = terms[rows // 2 :].reshape(oth_out.shape)


def adapter_terms(low, left, right):
    return pl.pallas_call(
        term_kernel,
        grid=(NZ,),
        in_specs=[low_spec(), left_spec(), right_spec()],
        out_specs=[slot_spec(), slot_spec()],
        out_shape=[jax.ShapeDtypeStruct((NZ, NX, GROUP_ROWS, WIDE), BF)] * 2,
        compiler_params=params(),
        name="adapter_terms",
    )(low, left, right)


def finish_kernel(codes, own, oth, both, weight, first, second):
    terms = jnp.concatenate([own[...].reshape(SLOTS, WIDE), oth[...].reshape(SLOTS, WIDE)], axis=0)
    rows = dot_tn(one_hot(codes[0]), terms)
    inner = (rows[:, :MS] + dot_t(both[0, :, MS:], weight[...])).astype(BF)
    outer = rows[:, MS:].astype(BF)
    for at, out in ((0, first), (ROWS // 2, second)):
        out[0, :, :MS] = inner[at : at + ROWS // 2]
        out[0, :, MS:] = outer[at : at + ROWS // 2]


def finish(codes, own, oth, both, weight):
    slots = pl.BlockSpec((NZ, 1, GROUP_ROWS, WIDE), lambda i: (0, i, 0, 0))
    return pl.pallas_call(
        finish_kernel,
        grid=(NX,),
        in_specs=[
            pl.BlockSpec((1, 1, ROWS), lambda i: (i, 0, 0)),
            slots,
            slots,
            pl.BlockSpec((1, ROWS, BOTH), lambda i: (i, 0, 0)),
            pl.BlockSpec((MS, KV), lambda i: (0, 0)),
        ],
        out_specs=[pl.BlockSpec((1, ROWS // 2, WIDE), lambda i: (i, 0, 0))] * 2,
        out_shape=[jax.ShapeDtypeStruct((NX, ROWS // 2, WIDE), BF)] * 2,
        compiler_params=params(30),
        name="token_gradient",
    )(codes, own, oth, both, weight)


def pack_kernel(tok, cot, out):
    out[0, :, :MS] = tok[...]
    out[0, :, MS:] = cot[...]


def pack(tokens, cotangent):
    return pl.pallas_call(
        pack_kernel,
        grid=(NX,),
        in_specs=[
            pl.BlockSpec((ROWS, MS), lambda i: (0, i)),
            pl.BlockSpec((ROWS, KV), lambda i: (0, 0)),
        ],
        out_specs=pl.BlockSpec((1, ROWS, BOTH), lambda i: (i, 0, 0)),
        out_shape=jax.ShapeDtypeStruct((NX, ROWS, BOTH), BF),
        compiler_params=params(),
        name="pack_rows",
    )(tokens, cotangent)


def unpack_kernel(first, second, base, output, gradient):
    for at, half in ((0, first), (ROWS // 2, second)):
        rows = slice(at, at + ROWS // 2)
        gradient[rows, :] = half[0, :, :MS]
        summed = half[0, :, MS:].astype(F32)
        for k in range(NX):
            summed = summed + base[k, rows, :].astype(F32)
        output[rows, :] = summed.astype(BF)


def unpack(first, second, base):
    half = pl.BlockSpec((1, ROWS // 2, WIDE), lambda i: (i, 0, 0))
    return pl.pallas_call(
        unpack_kernel,
        grid=(NX,),
        in_specs=[half, half, pl.BlockSpec((NX, ROWS, KS), lambda i: (0, 0, i))],
        out_specs=[
            pl.BlockSpec((ROWS, KS), lambda i: (0, i)),
            pl.BlockSpec((ROWS, MS), lambda i: (0, i)),
        ],
        out_shape=[
            jax.ShapeDtypeStruct((ROWS, KV), BF),
            jax.ShapeDtypeStruct((ROWS, MODEL), BF),
        ],
        compiler_params=params(),
        name="unpack_rows",
    )(first, second, base)


def local(
    tokens,
    cotangent,
    tenant,
    adapter_per_slot,
    frozen_value_weight,
    down_factors,
    up_factors,
    down_first_moment,
    down_second_moment,
    up_first_moment,
    up_second_moment,
):
    x, y, z, c = (lax.axis_index(name) for name in ("x", "y", "z", "c"))

    wide = jnp.concatenate([down_factors[0].astype(BF).T, up_factors[0].astype(BF)], axis=1)

    matches = (tenant == adapter_per_slot[None, :]).astype(jnp.int32)
    earlier = jnp.cumsum(matches, axis=0) - matches
    place = jnp.sum(matches * earlier, axis=1)
    owner = jnp.sum(matches * jnp.arange(NY * NZ * NC, dtype=jnp.int32)[None, :], axis=1)
    core = (owner + c) % NC
    far = (y - owner // (NZ * NC)) % NY
    code = core * SLOTS + owner // NC % NZ * GROUP_ROWS + far * CAP + place
    codes = lax.all_gather(code.reshape(1, ROWS), "x", axis=0)

    left, right, rows = gather_weights(wide, z, pack(tokens, cotangent))
    base = jnp.einsum("srk,kn->srn", rows[:, :, :MS], frozen_value_weight, preferred_element_type=F32)

    own, sent = spread(x.reshape(1), codes, rows)
    oth = other_core(sent)
    low = sum_over_x(low_partial(own, oth, left, right))
    low, base = lax.optimization_barrier((low, base.astype(BF)))
    base = exchange(base, "x")
    own_terms, sent = adapter_terms(low, left, right)
    low, own_terms, sent = lax.optimization_barrier((low, own_terms, sent))
    oth_terms = other_core(sent)
    grad_left, grad_right = adapter_gradients(low, own, oth)
    first, second = finish(codes, own_terms, oth_terms, rows, frozen_value_weight)
    first, second, base = lax.optimization_barrier((first, second, base))
    gradient, first = scatter_gradients(grad_left, grad_right, z, second, exchange(first, "x"))
    second, first = lax.optimization_barrier((second, first))
    output, token_gradient = unpack(first, exchange(second, "x"), base)

    next_down_factors, next_down_first, next_down_second = moment_update(
        down_factors, down_first_moment, down_second_moment, gradient[:, :MS].T[None]
    )
    next_up_factors, next_up_first, next_up_second = moment_update(
        up_factors, up_first_moment, up_second_moment, gradient[:, MS:][None]
    )
    return (
        output,
        token_gradient,
        next_down_factors,
        next_up_factors,
        next_down_first,
        next_down_second,
        next_up_first,
        next_up_second,
    )


def solution(mesh):
    fine = Mesh(mesh.devices.reshape(NY, NZ, NC, NX), ("y", "z", "c", "x"))
    dp = ("y", "z", "c")
    rows = P((*dp, "x"), None)
    down = P(dp, "x", None)
    up = P(dp, None, "x")
    return jax.shard_map(
        local,
        mesh=fine,
        in_specs=(rows, rows, rows, P(), P("x", None), down, up, down, down, up, up),
        out_specs=(rows, rows, down, up, down, down, up, up),
        check_vma=False,
    )
```

```python
import jax
import jax.numpy as jnp
from jax import lax
from jax.experimental import pallas as pl
from jax.experimental.pallas import tpu as pltpu
from jax.sharding import Mesh, PartitionSpec as P

ADAPTER_SCALE = 0.25
BETA_ONE = 0.9
BETA_TWO = 0.99
ADAM_STEP = 10.0
ADAM_RATE = 0.02
ADAM_EPS = 1e-08

NY, NZ, NC, NX = 4, 8, 2, 4
ROWS = 256
MODEL = 5120
KV = 1024
RANK = 64
MS = MODEL // NX
KS = KV // NX
WIDE = MS + KS
LEFT = 640
RIGHT = WIDE - LEFT
REST = MS - LEFT
CAP = 8
GROUP_ROWS = NY * CAP
SLOTS = NZ * GROUP_ROWS
COLS = NY * RANK
BF = jnp.bfloat16
F32 = jnp.float32


def exchange(array, axis):
    return lax.all_to_all(array, axis, split_axis=0, concat_axis=0, tiled=True)


def gather(array, axis, count):
    return exchange(jnp.broadcast_to(array[None], (count, *array.shape)), axis)


def total(array):
    return jnp.sum(array.astype(F32), axis=0)


def shift(count, step):
    return [(i, (i + step) % count) for i in range(count)]


def along_y(array, step):
    return lax.ppermute(array, "y", shift(NY, step))


def along_z(array, step):
    return lax.ppermute(array, "z", shift(NZ, step))


def along_x(array, step):
    return lax.ppermute(array, "x", shift(NX, step))


def other_core(array):
    return lax.ppermute(array, "c", shift(NC, 1))


def moment_update(master, first_moment, second_moment, gradient):
    first_new = BETA_ONE * first_moment + (1.0 - BETA_ONE) * gradient
    second_new = BETA_TWO * second_moment + (1.0 - BETA_TWO) * gradient * gradient
    first_hat = first_new / (1.0 - BETA_ONE**ADAM_STEP)
    second_hat = second_new / (1.0 - BETA_TWO**ADAM_STEP)
    updated = master - ADAM_RATE * first_hat / (jnp.sqrt(second_hat) + ADAM_EPS)
    return (updated, first_new, second_new)


def dot(a, b):
    return jnp.dot(a, b, preferred_element_type=F32)


def dot_t(a, b):
    return lax.dot_general(a, b, (((1,), (1,)), ((), ())), preferred_element_type=F32)


def dot_tn(a, b):
    return lax.dot_general(a, b, (((0,), (0,)), ((), ())), preferred_element_type=F32)


def gather_weights(wide, rows, cots):
    left, right = wide[:, :LEFT], wide[:, LEFT:]
    half, cut = NZ // 2, COLS // 2
    right = jnp.stack([right] + [along_y(right, k) for k in range(1, NY)]).reshape(COLS, RIGHT)
    left = jnp.stack([left] + [along_z(left, k) for k in range(1, NZ)])
    whole = [None] * NZ
    whole[0] = up = down = right
    for k in range(1, half):
        up = whole[k] = along_z(up, 1)
        down = whole[NZ - k] = along_z(down, -1)
        if k == 1:
            up, down, left = lax.optimization_barrier((up, down, left))
            one, three = along_y(left, 1), along_y(left, -1)
        if k == half - 2:
            up, down, rows, one, three = lax.optimization_barrier((up, down, rows, one, three))
    two = jnp.concatenate([along_y(one[:half], 1), along_y(three[half:], -1)])
    whole[half] = jnp.concatenate([along_z(up[:cut], 1), along_z(down[cut:], -1)])
    whole[half], cots = lax.optimization_barrier((whole[half], cots))
    return jnp.stack([left, one, two, three]), jnp.stack(whole), rows, cots


def add(a, b):
    return (a.astype(F32) + b.astype(F32)).astype(BF)


def add_half(a, b, low):
    half = a.shape[0] // 2
    if low:
        return jnp.concatenate([add(a[:half], b), a[half:]])
    return jnp.concatenate([a[:half], add(a[half:], b)])


def start_scatter(left, right):
    half, cut = NZ // 2, COLS // 2
    ends = along_y(left[2][:half], -1), along_y(left[2][half:], 1)
    return (*ends, along_z(right[half][:cut], -1), along_z(right[half][cut:], 1))


def scatter_gradients(left, right, started, after, first):
    a, b, down, up = started
    one = along_y(add_half(left[1], a, True), -1)
    three = along_y(add_half(left[3], b, False), 1)
    down = along_z(add_half(right[3], down, True), -1)
    up = along_z(add_half(right[5], up, False), 1)
    down, up, one, three, _ = lax.optimization_barrier((down, up, one, three, after))
    down, up = along_z(add(down, right[2]), -1), along_z(add(up, right[6]), 1)
    left = (left[0].astype(F32) + one + three).astype(BF)
    far = [along_z(left[k], -k) for k in range(1, NZ)]
    down, up, first = lax.optimization_barrier((down, up, first))
    down, up = along_z(add(down, right[1]), -1), along_z(add(up, right[7]), 1)
    right = (right[0].astype(F32) + down + up).astype(BF).reshape(NY, RANK, RIGHT)
    near = [along_y(right[k], -k) for k in range(1, NY)]
    left, right = left[0].astype(F32), right[0].astype(F32)
    for part in far:
        left = left + part
    for part in near:
        right = right + part
    return jnp.concatenate([left, right], axis=1), first


def params(megabytes=20):
    return pltpu.CompilerParams(vmem_limit_bytes=megabytes * 1024 * 1024)


def one_hot(codes):
    slots = lax.broadcasted_iota(jnp.int32, (NC * SLOTS, ROWS), 0)
    return (slots == codes).astype(BF)


def spread_kernel(codes, rows, own, oth):
    placed = dot(one_hot(codes[0]), rows[0]).astype(BF)
    own[...] = placed[:SLOTS].reshape(own.shape)
    oth[...] = placed[SLOTS:].reshape(oth.shape)


def spread(codes, rows):
    out = pl.BlockSpec((NZ, 1, GROUP_ROWS, WIDE), lambda i: (0, i, 0, 0))
    return pl.pallas_call(
        spread_kernel,
        grid=(NX,),
        in_specs=[
            pl.BlockSpec((1, 1, ROWS), lambda i: (i, 0, 0)),
            pl.BlockSpec((1, ROWS, WIDE), lambda i: (i, 0, 0)),
        ],
        out_specs=[out, out],
        out_shape=[jax.ShapeDtypeStruct((NZ, NX, GROUP_ROWS, WIDE), BF)] * 2,
        compiler_params=params(),
        name="spread_rows",
    )(codes, rows)


def row_mask():
    rows = lax.broadcasted_iota(jnp.int32, (2 * NX * GROUP_ROWS, COLS), 0)
    cols = lax.broadcasted_iota(jnp.int32, (2 * NX * GROUP_ROWS, COLS), 1)
    return lax.rem(rows, GROUP_ROWS) // CAP == cols // RANK


def fold(product, mask):
    kept = jnp.where(mask, product, 0.0)
    half = kept[:, : 2 * RANK] + kept[:, 2 * RANK :]
    return half + pltpu.roll(half, RANK, 1)


def low_kernel(own, oth, left, right, out):
    mask = row_mask()
    rows = 2 * NX * GROUP_ROWS
    s = jnp.concatenate(
        [own[...].reshape(rows // 2, WIDE), oth[...].reshape(rows // 2, WIDE)], axis=0
    )
    wl = left[...].reshape(COLS, LEFT)
    wr = right[...].reshape(COLS, RIGHT)
    low = dot_t(s[:, :LEFT], wl) + dot_t(s[:, LEFT:MS], wr[:, :REST])
    grad = dot_t(s[:, MS:], wr[:, REST:])
    lanes = lax.broadcasted_iota(jnp.int32, (rows, 2 * RANK), 1)
    out[0] = jnp.where(lanes < RANK, fold(low, mask), fold(grad, mask)).astype(BF)


def slot_spec():
    return pl.BlockSpec((1, NX, GROUP_ROWS, WIDE), lambda g: (g, 0, 0, 0))


def left_spec():
    return pl.BlockSpec((NY, 1, RANK, LEFT), lambda g: (0, g, 0, 0))


def right_spec():
    return pl.BlockSpec((1, COLS, RIGHT), lambda g: (g, 0, 0))


def low_spec():
    return pl.BlockSpec((1, 2 * NX * GROUP_ROWS, 2 * RANK), lambda g: (g, 0, 0))


def low_partial(own, oth, left, right):
    return pl.pallas_call(
        low_kernel,
        grid=(NZ,),
        in_specs=[slot_spec(), slot_spec(), left_spec(), right_spec()],
        out_specs=low_spec(),
        out_shape=jax.ShapeDtypeStruct((NZ, 2 * NX * GROUP_ROWS, 2 * RANK), BF),
        compiler_params=params(),
        name="low_partial",
    )(own, oth, left, right)


def sum_over_x(partial):
    share = NZ // NX
    parts = exchange(partial.reshape(NX, share, *partial.shape[1:]), "x")
    mine = (ADAPTER_SCALE * total(parts)).astype(BF)
    return gather(mine, "x", NX).reshape(partial.shape)


def masked(low):
    mask = row_mask()
    both = low.astype(F32)
    turned = pltpu.roll(both, RANK, 1)
    lanes = lax.broadcasted_iota(jnp.int32, both.shape, 1)
    reduced = jnp.where(lanes < RANK, both, turned)
    gradient = jnp.where(lanes < RANK, turned, both)
    reduced = jnp.where(mask, jnp.concatenate([reduced, reduced], axis=1), 0.0).astype(BF)
    gradient = jnp.where(mask, jnp.concatenate([gradient, gradient], axis=1), 0.0).astype(BF)
    return reduced, gradient


def gradient_kernel(low, own, oth, grad_left, grad_right):
    rows = 2 * NX * GROUP_ROWS
    s = jnp.concatenate(
        [own[...].reshape(rows // 2, WIDE), oth[...].reshape(rows // 2, WIDE)], axis=0
    )
    reduced, gradient = masked(low[0])
    grad_left[...] = dot_tn(gradient, s[:, :LEFT]).astype(BF).reshape(grad_left.shape)
    grad_right[0, :, :REST] = dot_tn(gradient, s[:, LEFT:MS]).astype(BF)
    grad_right[0, :, REST:] = dot_tn(reduced, s[:, MS:]).astype(BF)


def adapter_gradients(low, own, oth):
    return pl.pallas_call(
        gradient_kernel,
        grid=(NZ,),
        in_specs=[low_spec(), slot_spec(), slot_spec()],
        out_specs=[left_spec(), right_spec()],
        out_shape=[
            jax.ShapeDtypeStruct((NY, NZ, RANK, LEFT), BF),
            jax.ShapeDtypeStruct((NZ, COLS, RIGHT), BF),
        ],
        compiler_params=params(),
        name="adapter_gradients",
    )(low, own, oth)


def term_kernel(low, left, right, own_out, oth_out):
    rows = 2 * NX * GROUP_ROWS
    wl = left[...].reshape(COLS, LEFT)
    wr = right[...].reshape(COLS, RIGHT)
    reduced, gradient = masked(low[0])
    terms = jnp.concatenate(
        [
            dot(gradient, wl).astype(BF),
            dot(gradient, wr[:, :REST]).astype(BF),
            dot(reduced, wr[:, REST:]).astype(BF),
        ],
        axis=1,
    )
    own_out[...] = terms[: rows // 2].reshape(own_out.shape)
    oth_out[...] = terms[rows // 2 :].reshape(oth_out.shape)


def adapter_terms(low, left, right):
    return pl.pallas_call(
        term_kernel,
        grid=(NZ,),
        in_specs=[low_spec(), left_spec(), right_spec()],
        out_specs=[slot_spec(), slot_spec()],
        out_shape=[jax.ShapeDtypeStruct((NZ, NX, GROUP_ROWS, WIDE), BF)] * 2,
        compiler_params=params(),
        name="adapter_terms",
    )(low, left, right)


def finish_kernel(codes, own, oth, cot, weight, first, second):
    terms = jnp.concatenate([own[...].reshape(SLOTS, WIDE), oth[...].reshape(SLOTS, WIDE)], axis=0)
    rows = dot_tn(one_hot(codes[0]), terms)
    inner = (rows[:, :MS] + dot_t(cot[0], weight[...])).astype(BF)
    outer = rows[:, MS:].astype(BF)
    for at, out in ((0, first), (ROWS // 2, second)):
        out[0, :, :MS] = inner[at : at + ROWS // 2]
        out[0, :, MS:] = outer[at : at + ROWS // 2]


def finish(codes, own, oth, cots, weight):
    slots = pl.BlockSpec((NZ, 1, GROUP_ROWS, WIDE), lambda i: (0, i, 0, 0))
    return pl.pallas_call(
        finish_kernel,
        grid=(NX,),
        in_specs=[
            pl.BlockSpec((1, 1, ROWS), lambda i: (i, 0, 0)),
            slots,
            slots,
            pl.BlockSpec((1, ROWS, KV), lambda i: (i, 0, 0)),
            pl.BlockSpec((MS, KV), lambda i: (0, 0)),
        ],
        out_specs=[pl.BlockSpec((1, ROWS // 2, WIDE), lambda i: (i, 0, 0))] * 2,
        out_shape=[jax.ShapeDtypeStruct((NX, ROWS // 2, WIDE), BF)] * 2,
        compiler_params=params(30),
        name="token_gradient",
    )(codes, own, oth, cots, weight)


def pack_kernel(tok, cot, out):
    out[0, :, :MS] = tok[...]
    out[0, :, MS:] = cot[...]


def pack(tokens, cotangent):
    return pl.pallas_call(
        pack_kernel,
        grid=(NX,),
        in_specs=[
            pl.BlockSpec((ROWS, MS), lambda i: (0, i)),
            pl.BlockSpec((ROWS, KS), lambda i: (0, i)),
        ],
        out_specs=pl.BlockSpec((1, ROWS, WIDE), lambda i: (i, 0, 0)),
        out_shape=jax.ShapeDtypeStruct((NX, ROWS, WIDE), BF),
        compiler_params=params(),
        name="pack_rows",
    )(tokens, cotangent)


def unpack_kernel(first, second, b0, b1, b2, b3, output, gradient):
    for at, half in ((0, first), (ROWS // 2, second)):
        rows = slice(at, at + ROWS // 2)
        gradient[rows, :] = half[0, :, :MS]
        summed = half[0, :, MS:].astype(F32)
        for part in (b0, b1, b2, b3):
            summed = summed + part[rows, :].astype(F32)
        output[rows, :] = summed.astype(BF)


def unpack(first, second, base):
    half = pl.BlockSpec((1, ROWS // 2, WIDE), lambda i: (i, 0, 0))
    return pl.pallas_call(
        unpack_kernel,
        grid=(NX,),
        in_specs=[half, half] + [pl.BlockSpec((ROWS, KS), lambda i: (0, i))] * NX,
        out_specs=[
            pl.BlockSpec((ROWS, KS), lambda i: (0, i)),
            pl.BlockSpec((ROWS, MS), lambda i: (0, i)),
        ],
        out_shape=[
            jax.ShapeDtypeStruct((ROWS, KV), BF),
            jax.ShapeDtypeStruct((ROWS, MODEL), BF),
        ],
        compiler_params=params(),
        name="unpack_rows",
    )(first, second, *base)


def local(
    tokens,
    cotangent,
    tenant,
    adapter_per_slot,
    frozen_value_weight,
    down_factors,
    up_factors,
    down_first_moment,
    down_second_moment,
    up_first_moment,
    up_second_moment,
):
    x, y, z, c = (lax.axis_index(name) for name in ("x", "y", "z", "c"))

    wide = jnp.concatenate([down_factors[0].astype(BF).T, up_factors[0].astype(BF)], axis=1)

    matches = (tenant == adapter_per_slot[None, :]).astype(jnp.int32)
    earlier = jnp.cumsum(matches, axis=0) - matches
    place = jnp.sum(matches * earlier, axis=1)
    owner = jnp.sum(matches * jnp.arange(NY * NZ * NC, dtype=jnp.int32)[None, :], axis=1)
    core = (owner + c) % NC
    far_y = (y - owner // (NZ * NC)) % NY
    far_z = (z - owner // NC % NZ) % NZ
    code = (core * SLOTS + far_z * GROUP_ROWS + far_y * CAP + place).reshape(1, ROWS)
    codes = jnp.stack([code] + [along_x(code, k) for k in range(1, NX)])
    codes = jnp.take(codes, (x - jnp.arange(NX)) % NX, axis=0)

    rows = exchange(pack(tokens, cotangent), "x")
    cots = gather(cotangent, "x", NX)
    left, right, rows, cots = gather_weights(wide, rows, cots)
    base = jnp.einsum("srk,kn->srn", rows[:, :, :MS], frozen_value_weight, preferred_element_type=F32)
    base = base.astype(BF)
    base = [
        lax.dynamic_index_in_dim(base, (x + k) % NX, 0, keepdims=False) for k in range(NX)
    ]
    base = [base[0]] + [along_x(base[k], k) for k in range(1, NX)]

    own, sent = spread(codes, rows)
    oth = other_core(sent)
    oth, base[1], base[3] = lax.optimization_barrier((oth, base[1], base[3]))
    low = sum_over_x(low_partial(own, oth, left, right))
    own_terms, sent = adapter_terms(low, left, right)
    low, own_terms, sent = lax.optimization_barrier((low, own_terms, sent))
    oth_terms = other_core(sent)
    grad_left, grad_right = adapter_gradients(low, own, oth)
    started = start_scatter(grad_left, grad_right)
    first, second = finish(codes, own_terms, oth_terms, cots, frozen_value_weight)
    first, *base = lax.optimization_barrier((first, *base))
    first = exchange(first, "x")
    gradient, first = scatter_gradients(grad_left, grad_right, started, second, first)
    second, first = lax.optimization_barrier((second, first))
    output, token_gradient = unpack(first, exchange(second, "x"), base)

    next_down_factors, next_down_first, next_down_second = moment_update(
        down_factors, down_first_moment, down_second_moment, gradient[:, :MS].T[None]
    )
    next_up_factors, next_up_first, next_up_second = moment_update(
        up_factors, up_first_moment, up_second_moment, gradient[:, MS:][None]
    )
    return (
        output,
        token_gradient,
        next_down_factors,
        next_up_factors,
        next_down_first,
        next_down_second,
        next_up_first,
        next_up_second,
    )


def solution(mesh):
    fine = Mesh(mesh.devices.reshape(NY, NZ, NC, NX), ("y", "z", "c", "x"))
    dp = ("y", "z", "c")
    rows = P((*dp, "x"), None)
    down = P(dp, "x", None)
    up = P(dp, None, "x")
    return jax.shard_map(
        local,
        mesh=fine,
        in_specs=(rows, rows, rows, P(), P("x", None), down, up, down, down, up, up),
        out_specs=(rows, rows, down, up, down, down, up, up),
        check_vma=False,
    )
```

```python
import jax
import jax.numpy as jnp
from jax import lax
from jax.experimental import pallas as pl
from jax.experimental.pallas import tpu as pltpu
from jax.sharding import Mesh, PartitionSpec as P

ADAPTER_SCALE = 0.25
BETA_ONE = 0.9
BETA_TWO = 0.99
ADAM_STEP = 10.0
ADAM_RATE = 0.02
ADAM_EPS = 1e-08

NY, NZ, NC, NX = 4, 8, 2, 4
ROWS = 256
MODEL = 5120
KV = 1024
RANK = 64
MS = MODEL // NX
KS = KV // NX
WIDE = MS + KS
LEFT = 768
RIGHT = WIDE - LEFT
REST = MS - LEFT
CODE = 128
SENT = WIDE + CODE
CAP = 8
GROUP_ROWS = NY * CAP
SLOTS = NZ * GROUP_ROWS
COLS = NY * RANK
BF = jnp.bfloat16
F32 = jnp.float32


def exchange(array, axis):
    return lax.all_to_all(array, axis, split_axis=0, concat_axis=0, tiled=True)


def gather(array, axis, count):
    return exchange(jnp.broadcast_to(array[None], (count, *array.shape)), axis)


def total(array):
    return jnp.sum(array.astype(F32), axis=0)


def shift(count, step):
    return [(i, (i + step) % count) for i in range(count)]


def along_y(array, step):
    return lax.ppermute(array, "y", shift(NY, step))


def along_z(array, step):
    return lax.ppermute(array, "z", shift(NZ, step))


def along_x(array, step):
    return lax.ppermute(array, "x", shift(NX, step))


def other_core(array):
    return lax.ppermute(array, "c", shift(NC, 1))


def moment_update(master, first_moment, second_moment, gradient):
    first_new = BETA_ONE * first_moment + (1.0 - BETA_ONE) * gradient
    second_new = BETA_TWO * second_moment + (1.0 - BETA_TWO) * gradient * gradient
    first_hat = first_new / (1.0 - BETA_ONE**ADAM_STEP)
    second_hat = second_new / (1.0 - BETA_TWO**ADAM_STEP)
    updated = master - ADAM_RATE * first_hat / (jnp.sqrt(second_hat) + ADAM_EPS)
    return (updated, first_new, second_new)


def dot(a, b):
    return jnp.dot(a, b, preferred_element_type=F32)


def dot_t(a, b):
    return lax.dot_general(a, b, (((1,), (1,)), ((), ())), preferred_element_type=F32)


def dot_tn(a, b):
    return lax.dot_general(a, b, (((0,), (0,)), ((), ())), preferred_element_type=F32)


def put(whole, part, at):
    return lax.dynamic_update_slice_in_dim(whole, part[None], at, 0)


def gather_weights(wide, rows, y, z):
    left, right = wide[:, :LEFT], wide[:, LEFT:]
    half, cut = NZ // 2, COLS // 2
    left = lax.all_gather(left, ("y", "z"), axis=0).reshape(NY, NZ, RANK, LEFT)
    by_y = put(jnp.zeros((NY, RANK, RIGHT), BF), right, y)
    for k in range(1, NY):
        by_y = put(by_y, along_y(right, k), (y - k) % NY)
    up = down = by_y.reshape(COLS, RIGHT)
    whole = put(jnp.zeros((NZ, COLS, RIGHT), BF), up, z)
    for k in range(1, half):
        up, down = along_z(up, 1), along_z(down, -1)
        whole = put(put(whole, up, (z - k) % NZ), down, (z + k) % NZ)
    far = jnp.concatenate([along_z(up[:cut], 1), along_z(down[cut:], -1)])
    far, rows = lax.optimization_barrier((far, rows))
    return left, put(whole, far, (z + half) % NZ), rows


def add(a, b):
    return (a.astype(F32) + b.astype(F32)).astype(BF)


def add_half(a, b, low):
    half = a.shape[0] // 2
    if low:
        return jnp.concatenate([add(a[:half], b), a[half:]])
    return jnp.concatenate([a[:half], add(a[half:], b)])


def part(array, at, count):
    return lax.dynamic_index_in_dim(array, at % count, 0, keepdims=False)


def scatter_gradients(left, right, y, z, done):
    half, cut = NZ // 2, COLS // 2
    left = exchange(left, "y")
    far = part(right, z + half, NZ)
    down, up = along_z(far[:cut], -1), along_z(far[cut:], 1)
    down = along_z(add_half(part(right, z - 3, NZ), down, True), -1)
    up = along_z(add_half(part(right, z + 3, NZ), up, False), 1)
    down, up, *done[1:] = lax.optimization_barrier((down, up, *done[1:]))
    done = [done[0]] + [along_x(done[k], -k) for k in range(1, NX)]
    down = along_z(add(down, part(right, z - 2, NZ)), -1)
    up = along_z(add(up, part(right, z + 2, NZ)), 1)
    down, up, left, done[1], done[3] = lax.optimization_barrier((down, up, left, done[1], done[3]))
    left = exchange(total(left).astype(BF), "z")
    down = along_z(add(down, part(right, z - 1, NZ)), -1)
    up = along_z(add(up, part(right, z + 1, NZ)), 1)
    right = part(right, z, NZ).astype(F32) + down + up
    right = right.astype(BF).reshape(NY, RANK, RIGHT)
    near = [along_y(part(right, y - k, NY), -k) for k in range(1, NY)]
    right = part(right, y, NY).astype(F32) + near[0] + near[1] + near[2]
    return jnp.concatenate([total(left), right], axis=1), done


def params(megabytes=20):
    return pltpu.CompilerParams(vmem_limit_bytes=megabytes * 1024 * 1024)


def one_hot(code):
    code = code.astype(F32)
    slot = code[:, 0:1] * GROUP_ROWS + code[:, 1:2]
    slots = lax.broadcasted_iota(jnp.int32, (ROWS, NC * SLOTS), 1).astype(F32)
    return jnp.where(slots == slot, 1.0, 0.0).astype(BF)


def spread_kernel(rows, own, oth):
    placed = dot_tn(one_hot(rows[0, :, WIDE:]), rows[0, :, :WIDE]).astype(BF)
    own[...] = placed[:SLOTS].reshape(own.shape)
    oth[...] = placed[SLOTS:].reshape(oth.shape)


def spread(rows):
    out = pl.BlockSpec((NZ, 1, GROUP_ROWS, WIDE), lambda i: (0, i, 0, 0))
    return pl.pallas_call(
        spread_kernel,
        grid=(NX,),
        in_specs=[pl.BlockSpec((1, ROWS, SENT), lambda i: (i, 0, 0))],
        out_specs=[out, out],
        out_shape=[jax.ShapeDtypeStruct((NZ, NX, GROUP_ROWS, WIDE), BF)] * 2,
        compiler_params=params(),
        name="spread_rows",
    )(rows)


def row_mask():
    rows = lax.broadcasted_iota(jnp.int32, (2 * NX * GROUP_ROWS, COLS), 0)
    cols = lax.broadcasted_iota(jnp.int32, (2 * NX * GROUP_ROWS, COLS), 1)
    return lax.rem(rows, GROUP_ROWS) // CAP == cols // RANK


def fold(product, mask):
    kept = jnp.where(mask, product, 0.0)
    half = kept[:, : 2 * RANK] + kept[:, 2 * RANK :]
    return half + pltpu.roll(half, RANK, 1)


def low_kernel(own, oth, left, right, out):
    mask = row_mask()
    rows = 2 * NX * GROUP_ROWS
    s = jnp.concatenate(
        [own[...].reshape(rows // 2, WIDE), oth[...].reshape(rows // 2, WIDE)], axis=0
    )
    wl = left[...].reshape(COLS, LEFT)
    wr = right[...].reshape(COLS, RIGHT)
    low = dot_t(s[:, :LEFT], wl) + dot_t(s[:, LEFT:MS], wr[:, :REST])
    grad = dot_t(s[:, MS:], wr[:, REST:])
    lanes = lax.broadcasted_iota(jnp.int32, (rows, 2 * RANK), 1)
    out[0] = jnp.where(lanes < RANK, fold(low, mask), fold(grad, mask)).astype(BF)


def slot_spec():
    return pl.BlockSpec((1, NX, GROUP_ROWS, WIDE), lambda g: (g, 0, 0, 0))


def left_spec():
    return pl.BlockSpec((NY, 1, RANK, LEFT), lambda g: (0, g, 0, 0))


def right_spec():
    return pl.BlockSpec((1, COLS, RIGHT), lambda g: (g, 0, 0))


def low_spec():
    return pl.BlockSpec((1, 2 * NX * GROUP_ROWS, 2 * RANK), lambda g: (g, 0, 0))


def low_partial(own, oth, left, right):
    return pl.pallas_call(
        low_kernel,
        grid=(NZ,),
        in_specs=[slot_spec(), slot_spec(), left_spec(), right_spec()],
        out_specs=low_spec(),
        out_shape=jax.ShapeDtypeStruct((NZ, 2 * NX * GROUP_ROWS, 2 * RANK), BF),
        compiler_params=params(),
        name="low_partial",
    )(own, oth, left, right)


def sum_over_x(partial):
    share = NZ // NX
    parts = exchange(partial.reshape(NX, share, *partial.shape[1:]), "x")
    mine = (ADAPTER_SCALE * total(parts)).astype(BF)
    return gather(mine, "x", NX).reshape(partial.shape)


def masked(low):
    mask = row_mask()
    both = low.astype(F32)
    turned = pltpu.roll(both, RANK, 1)
    lanes = lax.broadcasted_iota(jnp.int32, both.shape, 1)
    reduced = jnp.where(lanes < RANK, both, turned)
    gradient = jnp.where(lanes < RANK, turned, both)
    reduced = jnp.where(mask, jnp.concatenate([reduced, reduced], axis=1), 0.0).astype(BF)
    gradient = jnp.where(mask, jnp.concatenate([gradient, gradient], axis=1), 0.0).astype(BF)
    return reduced, gradient


def gradient_kernel(low, own, oth, grad_left, grad_right):
    rows = 2 * NX * GROUP_ROWS
    s = jnp.concatenate(
        [own[...].reshape(rows // 2, WIDE), oth[...].reshape(rows // 2, WIDE)], axis=0
    )
    reduced, gradient = masked(low[0])
    grad_left[...] = dot_tn(gradient, s[:, :LEFT]).astype(BF).reshape(grad_left.shape)
    grad_right[0, :, :REST] = dot_tn(gradient, s[:, LEFT:MS]).astype(BF)
    grad_right[0, :, REST:] = dot_tn(reduced, s[:, MS:]).astype(BF)


def adapter_gradients(low, own, oth):
    return pl.pallas_call(
        gradient_kernel,
        grid=(NZ,),
        in_specs=[low_spec(), slot_spec(), slot_spec()],
        out_specs=[left_spec(), right_spec()],
        out_shape=[
            jax.ShapeDtypeStruct((NY, NZ, RANK, LEFT), BF),
            jax.ShapeDtypeStruct((NZ, COLS, RIGHT), BF),
        ],
        compiler_params=params(),
        name="adapter_gradients",
    )(low, own, oth)


def term_kernel(low, left, right, own_out, oth_out):
    rows = 2 * NX * GROUP_ROWS
    wl = left[...].reshape(COLS, LEFT)
    wr = right[...].reshape(COLS, RIGHT)
    reduced, gradient = masked(low[0])
    terms = jnp.concatenate(
        [
            dot(gradient, wl).astype(BF),
            dot(gradient, wr[:, :REST]).astype(BF),
            dot(reduced, wr[:, REST:]).astype(BF),
        ],
        axis=1,
    )
    own_out[...] = terms[: rows // 2].reshape(own_out.shape)
    oth_out[...] = terms[rows // 2 :].reshape(oth_out.shape)


def adapter_terms(low, left, right):
    return pl.pallas_call(
        term_kernel,
        grid=(NZ,),
        in_specs=[low_spec(), left_spec(), right_spec()],
        out_specs=[slot_spec(), slot_spec()],
        out_shape=[jax.ShapeDtypeStruct((NZ, NX, GROUP_ROWS, WIDE), BF)] * 2,
        compiler_params=params(),
        name="adapter_terms",
    )(low, left, right)


def finish_kernel(x, code, own, oth, cot, weight, out):
    terms = jnp.concatenate([own[...].reshape(SLOTS, WIDE), oth[...].reshape(SLOTS, WIDE)], axis=0)
    rows = dot(one_hot(code[0]), terms)
    out[:, :MS] = (rows[:, :MS] + dot_t(cot[0], weight[...])).astype(BF)
    out[:, MS:] = rows[:, MS:].astype(BF)


def finish(k, x, rows, own, oth, cots, weight):
    slots = pl.BlockSpec((NZ, 1, GROUP_ROWS, WIDE), lambda i, x: (0, (x[0] + NX - k) % NX, 0, 0))
    return pl.pallas_call(
        finish_kernel,
        grid_spec=pltpu.PrefetchScalarGridSpec(
            num_scalar_prefetch=1,
            grid=(1,),
            in_specs=[
                pl.BlockSpec((1, ROWS, CODE), lambda i, x: ((x[0] + NX - k) % NX, 0, WIDE // CODE)),
                slots,
                slots,
                pl.BlockSpec((1, ROWS, KV), lambda i, x: ((x[0] + NX - k) % NX, 0, 0)),
                pl.BlockSpec((MS, KV), lambda i, x: (0, 0)),
            ],
            out_specs=pl.BlockSpec((ROWS, WIDE), lambda i, x: (0, 0)),
        ),
        out_shape=jax.ShapeDtypeStruct((ROWS, WIDE), BF),
        compiler_params=params(30),
        name="token_gradient",
    )(x, rows, own, oth, cots, weight)


def pack_kernel(tok, cot, code, out):
    out[0, :, :MS] = tok[...]
    out[0, :, MS:WIDE] = cot[...]
    out[0, :, WIDE:] = code[...]


def pack(tokens, cotangent, code):
    return pl.pallas_call(
        pack_kernel,
        grid=(NX,),
        in_specs=[
            pl.BlockSpec((ROWS, MS), lambda i: (0, i)),
            pl.BlockSpec((ROWS, KS), lambda i: (0, i)),
            pl.BlockSpec((ROWS, CODE), lambda i: (0, 0)),
        ],
        out_specs=pl.BlockSpec((1, ROWS, SENT), lambda i: (i, 0, 0)),
        out_shape=jax.ShapeDtypeStruct((NX, ROWS, SENT), BF),
        compiler_params=params(),
        name="pack_rows",
    )(tokens, cotangent, code)


def unpack_kernel(x, d0, d1, d2, d3, base, output, gradient):
    for k, done in enumerate((d0, d1, d2, d3)):
        at = lax.rem(x[0] + k, NX)
        wide = pl.ds(pl.multiple_of(at * MS, MS), MS)
        thin = pl.ds(pl.multiple_of(at * KS, KS), KS)
        gradient[:, wide] = done[:, :MS]
        output[:, thin] = (done[:, MS:].astype(F32) + base[:, thin].astype(F32)).astype(BF)


def unpack(x, done, base):
    def whole(columns):
        return pl.BlockSpec((ROWS, columns), lambda i, x: (0, 0))

    return pl.pallas_call(
        unpack_kernel,
        grid_spec=pltpu.PrefetchScalarGridSpec(
            num_scalar_prefetch=1,
            grid=(1,),
            in_specs=[whole(WIDE)] * NX + [whole(KV)],
            out_specs=[whole(KV), whole(MODEL)],
        ),
        out_shape=[
            jax.ShapeDtypeStruct((ROWS, KV), BF),
            jax.ShapeDtypeStruct((ROWS, MODEL), BF),
        ],
        compiler_params=params(30),
        name="unpack_rows",
    )(x, *done, base)


def local(
    tokens,
    cotangent,
    tenant,
    adapter_per_slot,
    frozen_value_weight,
    down_factors,
    up_factors,
    down_first_moment,
    down_second_moment,
    up_first_moment,
    up_second_moment,
):
    x, y, z, c = (lax.axis_index(name) for name in ("x", "y", "z", "c"))

    wide = jnp.concatenate([down_factors[0].astype(BF).T, up_factors[0].astype(BF)], axis=1)

    matches = (tenant == adapter_per_slot[None, :]).astype(jnp.int32)
    earlier = jnp.cumsum(matches, axis=0) - matches
    place = jnp.sum(matches * earlier, axis=1)
    owner = jnp.sum(matches * jnp.arange(NY * NZ * NC, dtype=jnp.int32)[None, :], axis=1)
    core = (owner + c) % NC
    high = (core * NZ + owner // NC % NZ)[:, None]
    low = (owner // (NZ * NC) * CAP + place)[:, None]
    code = jnp.concatenate([high, low, jnp.zeros((ROWS, CODE - 2), jnp.int32)], axis=1).astype(BF)

    rows = exchange(pack(tokens, cotangent, code), "x")
    left, right, rows = gather_weights(wide, rows, y, z)
    cots = gather(cotangent, "x", NX)
    base = jnp.einsum("srk,kn->srn", rows[:, :, :MS], frozen_value_weight, preferred_element_type=F32)
    base = base.astype(BF)

    own, sent = spread(rows)
    oth = other_core(sent)
    oth, base = lax.optimization_barrier((oth, base))
    base = lax.psum_scatter(base, "x", scatter_dimension=0, tiled=False)
    low, cots = lax.optimization_barrier((low_partial(own, oth, left, right), cots))
    low = sum_over_x(low)
    own_terms, sent = adapter_terms(low, left, right)
    low, own_terms, sent = lax.optimization_barrier((low, own_terms, sent))
    oth_terms = other_core(sent)
    grad_left, grad_right = adapter_gradients(low, own, oth)
    done = [None] * NX
    for k in (1, 3, 2, 0):
        done[k] = finish(k, x.reshape(1), rows, own_terms, oth_terms, cots, frozen_value_weight)
    gradient, done = scatter_gradients(grad_left, grad_right, y, z, done)
    output, token_gradient = unpack(x.reshape(1), done, base)

    next_down_factors, next_down_first, next_down_second = moment_update(
        down_factors, down_first_moment, down_second_moment, gradient[:, :MS].T[None]
    )
    next_up_factors, next_up_first, next_up_second = moment_update(
        up_factors, up_first_moment, up_second_moment, gradient[:, MS:][None]
    )
    return (
        output,
        token_gradient,
        next_down_factors,
        next_up_factors,
        next_down_first,
        next_down_second,
        next_up_first,
        next_up_second,
    )


def solution(mesh):
    fine = Mesh(mesh.devices.reshape(NY, NZ, NC, NX), ("y", "z", "c", "x"))
    dp = ("y", "z", "c")
    rows = P((*dp, "x"), None)
    down = P(dp, "x", None)
    up = P(dp, None, "x")
    return jax.shard_map(
        local,
        mesh=fine,
        in_specs=(rows, rows, rows, P(), P("x", None), down, up, down, down, up, up),
        out_specs=(rows, rows, down, up, down, down, up, up),
        check_vma=False,
    )
```

```python
import jax
import jax.numpy as jnp
from jax import lax
from jax.experimental import pallas as pl
from jax.experimental.pallas import tpu as pltpu
from jax.sharding import Mesh, PartitionSpec as P

ADAPTER_SCALE = 0.25
BETA_ONE = 0.9
BETA_TWO = 0.99
ADAM_STEP = 10.0
ADAM_RATE = 0.02
ADAM_EPS = 1e-08

NY, NZ, NC, NX = 4, 8, 2, 4
ROWS = 256
MODEL = 5120
KV = 1024
RANK = 64
MS = MODEL // NX
KS = KV // NX
WIDE = MS + KS
LEFT = 640
RIGHT = WIDE - LEFT
REST = MS - LEFT
CODE = 128
SENT = WIDE + CODE
CAP = 8
GROUP_ROWS = NY * CAP
SLOTS = NZ * GROUP_ROWS
COLS = NY * RANK
BF = jnp.bfloat16
F32 = jnp.float32


def exchange(array, axis):
    return lax.all_to_all(array, axis, split_axis=0, concat_axis=0, tiled=True)


def gather(array, axis, count):
    return exchange(jnp.broadcast_to(array[None], (count, *array.shape)), axis)


def total(array):
    return jnp.sum(array.astype(F32), axis=0)


def shift(count, step):
    return [(i, (i + step) % count) for i in range(count)]


def along_y(array, step):
    return lax.ppermute(array, "y", shift(NY, step))


def along_z(array, step):
    return lax.ppermute(array, "z", shift(NZ, step))


def along_x(array, step):
    return lax.ppermute(array, "x", shift(NX, step))


def other_core(array):
    return lax.ppermute(array, "c", shift(NC, 1))


def moment_update(master, first_moment, second_moment, gradient):
    first_new = BETA_ONE * first_moment + (1.0 - BETA_ONE) * gradient
    second_new = BETA_TWO * second_moment + (1.0 - BETA_TWO) * gradient * gradient
    first_hat = first_new / (1.0 - BETA_ONE**ADAM_STEP)
    second_hat = second_new / (1.0 - BETA_TWO**ADAM_STEP)
    updated = master - ADAM_RATE * first_hat / (jnp.sqrt(second_hat) + ADAM_EPS)
    return (updated, first_new, second_new)


def dot(a, b):
    return jnp.dot(a, b, preferred_element_type=F32)


def dot_t(a, b):
    return lax.dot_general(a, b, (((1,), (1,)), ((), ())), preferred_element_type=F32)


def dot_tn(a, b):
    return lax.dot_general(a, b, (((0,), (0,)), ((), ())), preferred_element_type=F32)


def gather_weights(wide):
    return lax.all_gather(wide, ("y", "z"), axis=0).reshape(NY, NZ, RANK, WIDE)


def part(array, at, count):
    return lax.dynamic_index_in_dim(array, at % count, 0, keepdims=False)


def scatter_gradients(left, right, y, done, last):
    left = exchange(left, "y")
    right = lax.psum_scatter(right, "z", scatter_dimension=0, tiled=False)
    second = done[2]
    done = [done[0]] + [along_x(done[k], -k) for k in range(1, NX)]
    left, second = lax.optimization_barrier((left, second))
    left, done[1], done[3], last = lax.optimization_barrier((left, done[1], done[3], last))
    left = exchange(total(left).astype(BF), "z")
    right = right.reshape(NY, RANK, RIGHT)
    near = [along_y(part(right, y - k, NY), -k) for k in range(1, NY)]
    right = part(right, y, NY).astype(F32) + near[0] + near[1] + near[2]
    return jnp.concatenate([total(left), right], axis=1), done, last


def params(megabytes=56):
    return pltpu.CompilerParams(vmem_limit_bytes=megabytes * 1024 * 1024)


def one_hot(code):
    code = code.astype(F32)
    slot = code[:, 0:1] * GROUP_ROWS + code[:, 1:2]
    slots = lax.broadcasted_iota(jnp.int32, (ROWS, NC * SLOTS), 1).astype(F32)
    return jnp.where(slots == slot, 1.0, 0.0).astype(BF)


def spread_kernel(x, r0, r1, r2, r3, own, oth):
    for k, rows in enumerate((r0, r1, r2, r3)):
        source = pl.ds(lax.rem(x[0] + NX - k, NX), 1)
        placed = dot_tn(one_hot(rows[:, WIDE:]), rows[:, :WIDE]).astype(BF)
        own[:, source] = placed[:SLOTS].reshape(NZ, 1, GROUP_ROWS, WIDE)
        oth[:, source] = placed[SLOTS:].reshape(NZ, 1, GROUP_ROWS, WIDE)


def spread(x, rows):
    out = pl.BlockSpec((NZ, NX, GROUP_ROWS, WIDE), lambda i, x: (0, 0, 0, 0))
    return pl.pallas_call(
        spread_kernel,
        grid_spec=pltpu.PrefetchScalarGridSpec(
            num_scalar_prefetch=1,
            grid=(1,),
            in_specs=[pl.BlockSpec((ROWS, SENT), lambda i, x: (0, 0))] * NX,
            out_specs=[out, out],
        ),
        out_shape=[jax.ShapeDtypeStruct((NZ, NX, GROUP_ROWS, WIDE), BF)] * 2,
        compiler_params=params(),
        name="spread_rows",
    )(x, *rows)


def row_mask():
    rows = lax.broadcasted_iota(jnp.int32, (2 * NX * GROUP_ROWS, COLS), 0)
    cols = lax.broadcasted_iota(jnp.int32, (2 * NX * GROUP_ROWS, COLS), 1)
    return lax.rem(rows, GROUP_ROWS) // CAP == cols // RANK


def fold(product, mask):
    kept = jnp.where(mask, product, 0.0)
    half = kept[:, : 2 * RANK] + kept[:, 2 * RANK :]
    return half + pltpu.roll(half, RANK, 1)


def low_kernel(own, oth, weights, out):
    mask = row_mask()
    rows = 2 * NX * GROUP_ROWS
    s = jnp.concatenate(
        [own[...].reshape(rows // 2, WIDE), oth[...].reshape(rows // 2, WIDE)], axis=0
    )
    w = weights[...].reshape(COLS, WIDE)
    low = dot_t(s[:, :MS], w[:, :MS])
    grad = dot_t(s[:, MS:], w[:, MS:])
    lanes = lax.broadcasted_iota(jnp.int32, (rows, 2 * RANK), 1)
    out[0] = jnp.where(lanes < RANK, fold(low, mask), fold(grad, mask)).astype(BF)


def slot_spec():
    return pl.BlockSpec((1, NX, GROUP_ROWS, WIDE), lambda g: (g, 0, 0, 0))


def left_spec(width=LEFT):
    return pl.BlockSpec((NY, 1, RANK, width), lambda g: (0, g, 0, 0))


def right_spec():
    return pl.BlockSpec((1, COLS, RIGHT), lambda g: (g, 0, 0))


def low_spec():
    return pl.BlockSpec((1, 2 * NX * GROUP_ROWS, 2 * RANK), lambda g: (g, 0, 0))


def low_partial(own, oth, weights):
    return pl.pallas_call(
        low_kernel,
        grid=(NZ,),
        in_specs=[slot_spec(), slot_spec(), left_spec(WIDE)],
        out_specs=low_spec(),
        out_shape=jax.ShapeDtypeStruct((NZ, 2 * NX * GROUP_ROWS, 2 * RANK), BF),
        compiler_params=params(),
        name="low_partial",
    )(own, oth, weights)


def sum_over_x(partial):
    share = NZ // NX
    parts = exchange(partial.reshape(NX, share, *partial.shape[1:]), "x")
    mine = (ADAPTER_SCALE * total(parts)).astype(BF)
    return gather(mine, "x", NX).reshape(partial.shape)


def masked(low):
    mask = row_mask()
    both = low.astype(F32)
    turned = pltpu.roll(both, RANK, 1)
    lanes = lax.broadcasted_iota(jnp.int32, both.shape, 1)
    reduced = jnp.where(lanes < RANK, both, turned)
    gradient = jnp.where(lanes < RANK, turned, both)
    reduced = jnp.where(mask, jnp.concatenate([reduced, reduced], axis=1), 0.0).astype(BF)
    gradient = jnp.where(mask, jnp.concatenate([gradient, gradient], axis=1), 0.0).astype(BF)
    return reduced, gradient


def gradient_kernel(low, own, oth, grad_left, grad_right):
    rows = 2 * NX * GROUP_ROWS
    s = jnp.concatenate(
        [own[...].reshape(rows // 2, WIDE), oth[...].reshape(rows // 2, WIDE)], axis=0
    )
    reduced, gradient = masked(low[0])
    grad_left[...] = dot_tn(gradient, s[:, :LEFT]).astype(BF).reshape(grad_left.shape)
    grad_right[0, :, :REST] = dot_tn(gradient, s[:, LEFT:MS]).astype(BF)
    grad_right[0, :, REST:] = dot_tn(reduced, s[:, MS:]).astype(BF)


def adapter_gradients(low, own, oth):
    return pl.pallas_call(
        gradient_kernel,
        grid=(NZ,),
        in_specs=[low_spec(), slot_spec(), slot_spec()],
        out_specs=[left_spec(), right_spec()],
        out_shape=[
            jax.ShapeDtypeStruct((NY, NZ, RANK, LEFT), BF),
            jax.ShapeDtypeStruct((NZ, COLS, RIGHT), BF),
        ],
        compiler_params=params(),
        name="adapter_gradients",
    )(low, own, oth)


def term_kernel(low, weights, own_out, oth_out):
    rows = 2 * NX * GROUP_ROWS
    w = weights[...].reshape(COLS, WIDE)
    reduced, gradient = masked(low[0])
    terms = jnp.concatenate(
        [dot(gradient, w[:, :MS]).astype(BF), dot(reduced, w[:, MS:]).astype(BF)], axis=1
    )
    own_out[...] = terms[: rows // 2].reshape(own_out.shape)
    oth_out[...] = terms[rows // 2 :].reshape(oth_out.shape)


def adapter_terms(low, weights):
    return pl.pallas_call(
        term_kernel,
        grid=(NZ,),
        in_specs=[low_spec(), left_spec(WIDE)],
        out_specs=[slot_spec(), slot_spec()],
        out_shape=[jax.ShapeDtypeStruct((NZ, NX, GROUP_ROWS, WIDE), BF)] * 2,
        compiler_params=params(),
        name="adapter_terms",
    )(low, weights)


def finish_kernel(x, code, own, oth, cot, weight, out):
    terms = jnp.concatenate([own[...].reshape(SLOTS, WIDE), oth[...].reshape(SLOTS, WIDE)], axis=0)
    rows = dot(one_hot(code[...]), terms)
    out[:, :MS] = (rows[:, :MS] + dot_t(cot[...], weight[...])).astype(BF)
    out[:, MS:] = rows[:, MS:].astype(BF)


def finish(k, x, rows, own, oth, cot, weight):
    slots = pl.BlockSpec((NZ, 1, GROUP_ROWS, WIDE), lambda i, x: (0, (x[0] + NX - k) % NX, 0, 0))
    return pl.pallas_call(
        finish_kernel,
        grid_spec=pltpu.PrefetchScalarGridSpec(
            num_scalar_prefetch=1,
            grid=(1,),
            in_specs=[
                pl.BlockSpec((ROWS, CODE), lambda i, x: (0, WIDE // CODE)),
                slots,
                slots,
                pl.BlockSpec((ROWS, KV), lambda i, x: (0, 0)),
                pl.BlockSpec((MS, KV), lambda i, x: (0, 0)),
            ],
            out_specs=pl.BlockSpec((ROWS, WIDE), lambda i, x: (0, 0)),
        ),
        out_shape=jax.ShapeDtypeStruct((ROWS, WIDE), BF),
        compiler_params=params(),
        name="token_gradient",
    )(x, rows, own, oth, cot, weight)


def pack_kernel(x, t0, t1, t2, t3, c0, c1, c2, c3, code, o0, o1, o2, o3):
    groups = zip((t0, t1, t2, t3), (c0, c1, c2, c3), (o0, o1, o2, o3), strict=True)
    for tok, cot, out in groups:
        out[:, :MS] = tok[...]
        out[:, MS:WIDE] = cot[...]
        out[:, WIDE:] = code[...]


def pack(x, tokens, cotangent, code):
    def columns(width, k):
        return pl.BlockSpec((ROWS, width), lambda i, x: (0, (x[0] + k) % NX))

    return pl.pallas_call(
        pack_kernel,
        grid_spec=pltpu.PrefetchScalarGridSpec(
            num_scalar_prefetch=1,
            grid=(1,),
            in_specs=[columns(MS, k) for k in range(NX)]
            + [columns(KS, k) for k in range(NX)]
            + [pl.BlockSpec((ROWS, CODE), lambda i, x: (0, 0))],
            out_specs=[pl.BlockSpec((ROWS, SENT), lambda i, x: (0, 0))] * NX,
        ),
        out_shape=[jax.ShapeDtypeStruct((ROWS, SENT), BF)] * NX,
        compiler_params=params(),
        name="pack_rows",
    )(x, *[tokens] * NX, *[cotangent] * NX, code)


def unpack_kernel(x, d0, d1, d2, d3, b0, b1, b2, b3, output, gradient):
    for k, done in enumerate((d0, d1, d2, d3)):
        at = lax.rem(x[0] + k, NX)
        wide = pl.ds(pl.multiple_of(at * MS, MS), MS)
        thin = pl.ds(pl.multiple_of(at * KS, KS), KS)
        gradient[:, wide] = done[:, :MS]
        summed = done[:, MS:].astype(F32)
        for base in (b0, b1, b2, b3):
            summed = summed + base[:, thin].astype(F32)
        output[:, thin] = summed.astype(BF)


def unpack(x, done, base):
    def whole(columns):
        return pl.BlockSpec((ROWS, columns), lambda i, x: (0, 0))

    return pl.pallas_call(
        unpack_kernel,
        grid_spec=pltpu.PrefetchScalarGridSpec(
            num_scalar_prefetch=1,
            grid=(1,),
            in_specs=[whole(WIDE)] * NX + [whole(KV)] * NX,
            out_specs=[whole(KV), whole(MODEL)],
        ),
        out_shape=[
            jax.ShapeDtypeStruct((ROWS, KV), BF),
            jax.ShapeDtypeStruct((ROWS, MODEL), BF),
        ],
        compiler_params=params(),
        name="unpack_rows",
    )(x, *done, *base)


def local(
    tokens,
    cotangent,
    tenant,
    adapter_per_slot,
    frozen_value_weight,
    down_factors,
    up_factors,
    down_first_moment,
    down_second_moment,
    up_first_moment,
    up_second_moment,
):
    x, y, z, c = (lax.axis_index(name) for name in ("x", "y", "z", "c"))

    wide = jnp.concatenate([down_factors[0].astype(BF).T, up_factors[0].astype(BF)], axis=1)

    matches = (tenant == adapter_per_slot[None, :]).astype(jnp.int32)
    earlier = jnp.cumsum(matches, axis=0) - matches
    place = jnp.sum(matches * earlier, axis=1)
    owner = jnp.sum(matches * jnp.arange(NY * NZ * NC, dtype=jnp.int32)[None, :], axis=1)
    core = (owner + c) % NC
    high = (core * NZ + owner // NC % NZ)[:, None]
    low = (owner // (NZ * NC) * CAP + place)[:, None]
    code = jnp.concatenate([high, low, jnp.zeros((ROWS, CODE - 2), jnp.int32)], axis=1).astype(BF)

    weights = gather_weights(wide)
    at_x = x.reshape(1)
    rows = pack(at_x, tokens, cotangent, code)
    rows = [rows[0]] + [along_x(rows[k], k) for k in range(1, NX)]
    cots = [cotangent] + [along_x(cotangent, k) for k in range(1, NX)]
    base = [dot(part[:, :MS], frozen_value_weight).astype(BF) for part in rows]

    own, sent = spread(at_x, rows)
    oth = other_core(sent)
    oth, base = lax.optimization_barrier((oth, base))
    base = [base[0]] + [along_x(base[k], -k) for k in range(1, NX)]
    oth, cots, base[1], base[3] = lax.optimization_barrier((oth, cots, base[1], base[3]))
    low = sum_over_x(low_partial(own, oth, weights))
    own_terms, sent = adapter_terms(low, weights)
    low, own_terms, sent = lax.optimization_barrier((low, own_terms, sent))
    oth_terms = other_core(sent)
    grad_left, grad_right = adapter_gradients(low, own, oth)
    done = [None] * NX
    for k in (1, 3, 2, 0):
        done[k] = finish(k, at_x, rows[k], own_terms, oth_terms, cots[k], frozen_value_weight)
    gradient, done, base[2] = scatter_gradients(grad_left, grad_right, y, done, base[2])
    output, token_gradient = unpack(at_x, done, base)

    next_down_factors, next_down_first, next_down_second = moment_update(
        down_factors, down_first_moment, down_second_moment, gradient[:, :MS].T[None]
    )
    next_up_factors, next_up_first, next_up_second = moment_update(
        up_factors, up_first_moment, up_second_moment, gradient[:, MS:][None]
    )
    return (
        output,
        token_gradient,
        next_down_factors,
        next_up_factors,
        next_down_first,
        next_down_second,
        next_up_first,
        next_up_second,
    )


def solution(mesh):
    fine = Mesh(mesh.devices.reshape(NY, NZ, NC, NX), ("y", "z", "c", "x"))
    dp = ("y", "z", "c")
    rows = P((*dp, "x"), None)
    down = P(dp, "x", None)
    up = P(dp, None, "x")
    return jax.shard_map(
        local,
        mesh=fine,
        in_specs=(rows, rows, rows, P(), P("x", None), down, up, down, down, up, up),
        out_specs=(rows, rows, down, up, down, down, up, up),
        check_vma=False,
    )
```

```python
import jax
import jax.numpy as jnp
from jax import lax
from jax.experimental import pallas as pl
from jax.experimental.pallas import tpu as pltpu
from jax.sharding import Mesh, PartitionSpec as P

ADAPTER_SCALE = 0.25
BETA_ONE = 0.9
BETA_TWO = 0.99
ADAM_STEP = 10.0
ADAM_RATE = 0.02
ADAM_EPS = 1e-08

NY, NZ, NC, NX = 4, 8, 2, 4
ROWS = 256
MODEL = 5120
KV = 1024
RANK = 64
MS = MODEL // NX
KS = KV // NX
WIDE = MS + KS
LEFT = 512
RIGHT = WIDE - LEFT
REST = MS - LEFT
CODE = 128
SENT = WIDE + CODE
PER = 2
CAP = 8
GROUP_ROWS = NY * CAP
SLOTS = NZ * GROUP_ROWS
COLS = NY * RANK
BF = jnp.bfloat16
F32 = jnp.float32


def exchange(array, axis):
    return lax.all_to_all(array, axis, split_axis=0, concat_axis=0, tiled=True)


def gather(array, axis, count):
    return exchange(jnp.broadcast_to(array[None], (count, *array.shape)), axis)


def total(array):
    return jnp.sum(array.astype(F32), axis=0)


def shift(count, step):
    return [(i, (i + step) % count) for i in range(count)]


def along_y(array, step):
    return lax.ppermute(array, "y", shift(NY, step))


def along_z(array, step):
    return lax.ppermute(array, "z", shift(NZ, step))


def along_x(array, step):
    return lax.ppermute(array, "x", shift(NX, step))


def other_core(array):
    return lax.ppermute(array, "c", shift(NC, 1))


def moment_update(master, first_moment, second_moment, gradient):
    first_new = BETA_ONE * first_moment + (1.0 - BETA_ONE) * gradient
    second_new = BETA_TWO * second_moment + (1.0 - BETA_TWO) * gradient * gradient
    first_hat = first_new / (1.0 - BETA_ONE**ADAM_STEP)
    second_hat = second_new / (1.0 - BETA_TWO**ADAM_STEP)
    updated = master - ADAM_RATE * first_hat / (jnp.sqrt(second_hat) + ADAM_EPS)
    return (updated, first_new, second_new)


def dot(a, b):
    return jnp.dot(a, b, preferred_element_type=F32)


def dot_t(a, b):
    return lax.dot_general(a, b, (((1,), (1,)), ((), ())), preferred_element_type=F32)


def dot_tn(a, b):
    return lax.dot_general(a, b, (((0,), (0,)), ((), ())), preferred_element_type=F32)


def gather_weights(wide):
    return lax.all_gather(wide, ("y", "z"), axis=0).reshape(NY, NZ, RANK, WIDE)


def part(array, at, count):
    return lax.dynamic_index_in_dim(array, at % count, 0, keepdims=False)


def scatter_gradients(left, right, y, done):
    left = exchange(left, "y")
    right = lax.psum_scatter(right, "z", scatter_dimension=0, tiled=False)
    half = ROWS // 2
    one, three = along_x(done[1], -1), along_x(done[3], -3)
    two, rest = along_x(done[2][:half], -2), along_x(done[2][half:], -2)
    left, one, two, three = lax.optimization_barrier((left, one, two, three))
    left = exchange(total(left).astype(BF), "z")
    right = right.reshape(NY, RANK, RIGHT)
    near = [along_y(part(right, y - k, NY), -k) for k in range(1, NY)]
    right = part(right, y, NY).astype(F32) + near[0] + near[1] + near[2]
    right, rest = lax.optimization_barrier((right, rest))
    done = [done[0], one, two, rest, three]
    return jnp.concatenate([total(left), right], axis=1), done


def params(megabytes=56):
    return pltpu.CompilerParams(vmem_limit_bytes=megabytes * 1024 * 1024)


def one_hot(code):
    code = code.astype(F32)
    slot = code[:, 0:1] * GROUP_ROWS + code[:, 1:2]
    slots = lax.broadcasted_iota(jnp.int32, (ROWS, NC * SLOTS), 1).astype(F32)
    return jnp.where(slots == slot, 1.0, 0.0).astype(BF)


def spread_kernel(x, r0, r1, r2, r3, own, oth):
    for k, rows in enumerate((r0, r1, r2, r3)):
        source = pl.ds(lax.rem(x[0] + NX - k, NX), 1)
        placed = dot_tn(one_hot(rows[:, WIDE:]), rows[:, :WIDE]).astype(BF)
        own[:, source] = placed[:SLOTS].reshape(NZ, 1, GROUP_ROWS, WIDE)
        oth[:, source] = placed[SLOTS:].reshape(NZ, 1, GROUP_ROWS, WIDE)


def spread(x, rows):
    out = pl.BlockSpec((NZ, NX, GROUP_ROWS, WIDE), lambda i, x: (0, 0, 0, 0))
    return pl.pallas_call(
        spread_kernel,
        grid_spec=pltpu.PrefetchScalarGridSpec(
            num_scalar_prefetch=1,
            grid=(1,),
            in_specs=[pl.BlockSpec((ROWS, SENT), lambda i, x: (0, 0))] * NX,
            out_specs=[out, out],
        ),
        out_shape=[jax.ShapeDtypeStruct((NZ, NX, GROUP_ROWS, WIDE), BF)] * 2,
        compiler_params=params(),
        name="spread_rows",
    )(x, *rows)


def row_mask():
    rows = lax.broadcasted_iota(jnp.int32, (2 * NX * GROUP_ROWS, COLS), 0)
    cols = lax.broadcasted_iota(jnp.int32, (2 * NX * GROUP_ROWS, COLS), 1)
    return lax.rem(rows, GROUP_ROWS) // CAP == cols // RANK


def fold(product, mask):
    kept = jnp.where(mask, product, 0.0)
    half = kept[:, : 2 * RANK] + kept[:, 2 * RANK :]
    return half + pltpu.roll(half, RANK, 1)


def group_rows(own, oth, j):
    shape = (NX * GROUP_ROWS, WIDE)
    return jnp.concatenate([own[j].reshape(shape), oth[j].reshape(shape)], axis=0)


def low_kernel(own, oth, weights, out):
    mask = row_mask()
    lanes = lax.broadcasted_iota(jnp.int32, out.shape[1:], 1)
    for j in range(PER):
        s = group_rows(own, oth, j)
        w = weights[:, j].reshape(COLS, WIDE)
        low = dot_t(s[:, :MS], w[:, :MS])
        grad = dot_t(s[:, MS:], w[:, MS:])
        out[j] = jnp.where(lanes < RANK, fold(low, mask), fold(grad, mask)).astype(BF)


def slot_spec():
    return pl.BlockSpec((PER, NX, GROUP_ROWS, WIDE), lambda g: (g, 0, 0, 0))


def left_spec(width=LEFT):
    return pl.BlockSpec((NY, PER, RANK, width), lambda g: (0, g, 0, 0))


def right_spec():
    return pl.BlockSpec((PER, COLS, RIGHT), lambda g: (g, 0, 0))


def low_spec():
    return pl.BlockSpec((PER, 2 * NX * GROUP_ROWS, 2 * RANK), lambda g: (g, 0, 0))


def low_partial(own, oth, weights):
    return pl.pallas_call(
        low_kernel,
        grid=(NZ // PER,),
        in_specs=[slot_spec(), slot_spec(), left_spec(WIDE)],
        out_specs=low_spec(),
        out_shape=jax.ShapeDtypeStruct((NZ, 2 * NX * GROUP_ROWS, 2 * RANK), BF),
        compiler_params=params(),
        name="low_partial",
    )(own, oth, weights)


def sum_over_x(partial):
    share = NZ // NX
    parts = exchange(partial.reshape(NX, share, *partial.shape[1:]), "x")
    mine = (ADAPTER_SCALE * total(parts)).astype(BF)
    return gather(mine, "x", NX).reshape(partial.shape)


def masked(low, mask):
    both = low.astype(F32)
    turned = pltpu.roll(both, RANK, 1)
    lanes = lax.broadcasted_iota(jnp.int32, both.shape, 1)
    reduced = jnp.where(lanes < RANK, both, turned)
    gradient = jnp.where(lanes < RANK, turned, both)
    reduced = jnp.where(mask, jnp.concatenate([reduced, reduced], axis=1), 0.0).astype(BF)
    gradient = jnp.where(mask, jnp.concatenate([gradient, gradient], axis=1), 0.0).astype(BF)
    return reduced, gradient


def gradient_kernel(low, own, oth, grad_left, grad_right):
    mask = row_mask()
    for j in range(PER):
        s = group_rows(own, oth, j)
        reduced, gradient = masked(low[j], mask)
        near = dot_tn(gradient, s[:, :LEFT]).astype(BF)
        grad_left[:, j] = near.reshape(NY, RANK, LEFT)
        grad_right[j, :, :REST] = dot_tn(gradient, s[:, LEFT:MS]).astype(BF)
        grad_right[j, :, REST:] = dot_tn(reduced, s[:, MS:]).astype(BF)


def adapter_gradients(low, own, oth):
    return pl.pallas_call(
        gradient_kernel,
        grid=(NZ // PER,),
        in_specs=[low_spec(), slot_spec(), slot_spec()],
        out_specs=[left_spec(), right_spec()],
        out_shape=[
            jax.ShapeDtypeStruct((NY, NZ, RANK, LEFT), BF),
            jax.ShapeDtypeStruct((NZ, COLS, RIGHT), BF),
        ],
        compiler_params=params(),
        name="adapter_gradients",
    )(low, own, oth)


def term_kernel(low, weights, own_out, oth_out):
    mask = row_mask()
    shape = (NX, GROUP_ROWS)
    for j in range(PER):
        w = weights[:, j].reshape(COLS, WIDE)
        reduced, gradient = masked(low[j], mask)
        parts = ((slice(0, MS), gradient), (slice(MS, WIDE), reduced))
        for columns, factor in parts:
            terms = dot(factor, w[:, columns]).astype(BF)
            half, width = terms.shape[0] // 2, terms.shape[1]
            own_out[j, :, :, columns] = terms[:half].reshape(*shape, width)
            oth_out[j, :, :, columns] = terms[half:].reshape(*shape, width)


def adapter_terms(low, weights):
    return pl.pallas_call(
        term_kernel,
        grid=(NZ // PER,),
        in_specs=[low_spec(), left_spec(WIDE)],
        out_specs=[slot_spec(), slot_spec()],
        out_shape=[jax.ShapeDtypeStruct((NZ, NX, GROUP_ROWS, WIDE), BF)] * 2,
        compiler_params=params(),
        name="adapter_terms",
    )(low, weights)


def finish_kernel(x, code, own, oth, cot, weight, out):
    terms = jnp.concatenate([own[...].reshape(SLOTS, WIDE), oth[...].reshape(SLOTS, WIDE)], axis=0)
    rows = dot(one_hot(code[...]), terms)
    out[:, :MS] = (rows[:, :MS] + dot_t(cot[...], weight[...])).astype(BF)
    out[:, MS:] = rows[:, MS:].astype(BF)


def finish(k, x, rows, own, oth, cot, weight):
    slots = pl.BlockSpec((NZ, 1, GROUP_ROWS, WIDE), lambda i, x: (0, (x[0] + NX - k) % NX, 0, 0))
    return pl.pallas_call(
        finish_kernel,
        grid_spec=pltpu.PrefetchScalarGridSpec(
            num_scalar_prefetch=1,
            grid=(1,),
            in_specs=[
                pl.BlockSpec((ROWS, CODE), lambda i, x: (0, WIDE // CODE)),
                slots,
                slots,
                pl.BlockSpec((ROWS, KV), lambda i, x: (0, 0)),
                pl.BlockSpec((MS, KV), lambda i, x: (0, 0)),
            ],
            out_specs=pl.BlockSpec((ROWS, WIDE), lambda i, x: (0, 0)),
        ),
        out_shape=jax.ShapeDtypeStruct((ROWS, WIDE), BF),
        compiler_params=params(),
        name="token_gradient",
    )(x, rows, own, oth, cot, weight)


def pack_kernel(x, t0, t1, t2, t3, c0, c1, c2, c3, code, o0, o1, o2, o3):
    groups = zip((t0, t1, t2, t3), (c0, c1, c2, c3), (o0, o1, o2, o3), strict=True)
    for tok, cot, out in groups:
        out[:, :MS] = tok[...]
        out[:, MS:WIDE] = cot[...]
        out[:, WIDE:] = code[...]


def pack(x, tokens, cotangent, code):
    def columns(width, k):
        return pl.BlockSpec((ROWS, width), lambda i, x: (0, (x[0] + k) % NX))

    return pl.pallas_call(
        pack_kernel,
        grid_spec=pltpu.PrefetchScalarGridSpec(
            num_scalar_prefetch=1,
            grid=(1,),
            in_specs=[columns(MS, k) for k in range(NX)]
            + [columns(KS, k) for k in range(NX)]
            + [pl.BlockSpec((ROWS, CODE), lambda i, x: (0, 0))],
            out_specs=[pl.BlockSpec((ROWS, SENT), lambda i, x: (0, 0))] * NX,
        ),
        out_shape=[jax.ShapeDtypeStruct((ROWS, SENT), BF)] * NX,
        compiler_params=params(),
        name="pack_rows",
    )(x, *[tokens] * NX, *[cotangent] * NX, code)


def unpack_kernel(x, d0, d1, d2, rest, d3, b0, b1, b2, b3, output, gradient):
    half = ROWS // 2
    for k, start, done in ((0, 0, d0), (1, 0, d1), (2, 0, d2), (2, half, rest), (3, 0, d3)):
        at = lax.rem(x[0] + k, NX)
        rows = slice(start, start + done.shape[0])
        wide = pl.ds(pl.multiple_of(at * MS, MS), MS)
        thin = pl.ds(pl.multiple_of(at * KS, KS), KS)
        gradient[rows, wide] = done[:, :MS]
        summed = done[:, MS:].astype(F32)
        for base in (b0, b1, b2, b3):
            summed = summed + base[rows, thin].astype(F32)
        output[rows, thin] = summed.astype(BF)


def unpack(x, done, base):
    def whole(columns, rows=ROWS):
        return pl.BlockSpec((rows, columns), lambda i, x: (0, 0))

    return pl.pallas_call(
        unpack_kernel,
        grid_spec=pltpu.PrefetchScalarGridSpec(
            num_scalar_prefetch=1,
            grid=(1,),
            in_specs=[whole(WIDE, part.shape[0]) for part in done] + [whole(KV)] * NX,
            out_specs=[whole(KV), whole(MODEL)],
        ),
        out_shape=[
            jax.ShapeDtypeStruct((ROWS, KV), BF),
            jax.ShapeDtypeStruct((ROWS, MODEL), BF),
        ],
        compiler_params=params(),
        name="unpack_rows",
    )(x, *done, *base)


def local(
    tokens,
    cotangent,
    tenant,
    adapter_per_slot,
    frozen_value_weight,
    down_factors,
    up_factors,
    down_first_moment,
    down_second_moment,
    up_first_moment,
    up_second_moment,
):
    x, y, z, c = (lax.axis_index(name) for name in ("x", "y", "z", "c"))

    wide = jnp.concatenate([down_factors[0].astype(BF).T, up_factors[0].astype(BF)], axis=1)

    matches = (tenant == adapter_per_slot[None, :]).astype(jnp.int32)
    earlier = jnp.cumsum(matches, axis=0) - matches
    place = jnp.sum(matches * earlier, axis=1)
    owner = jnp.sum(matches * jnp.arange(NY * NZ * NC, dtype=jnp.int32)[None, :], axis=1)
    core = (owner + c) % NC
    high = (core * NZ + owner // NC % NZ)[:, None]
    low = (owner // (NZ * NC) * CAP + place)[:, None]
    code = jnp.concatenate([high, low, jnp.zeros((ROWS, CODE - 2), jnp.int32)], axis=1).astype(BF)

    weights = gather_weights(wide)
    at_x = x.reshape(1)
    rows = pack(at_x, tokens, cotangent, code)
    rows = [rows[0]] + [along_x(rows[k], k) for k in range(1, NX)]
    cots = [cotangent] + [along_x(cotangent, k) for k in range(1, NX)]
    base = [dot(part[:, :MS], frozen_value_weight).astype(BF) for part in rows]

    own, sent = spread(at_x, rows)
    oth = other_core(sent)
    oth, base = lax.optimization_barrier((oth, base))
    base = [base[0]] + [along_x(base[k], -k) for k in range(1, NX)]
    oth, cots, base[1], base[3] = lax.optimization_barrier((oth, cots, base[1], base[3]))
    low = sum_over_x(low_partial(own, oth, weights))
    low, base[2] = lax.optimization_barrier((low, base[2]))
    grad_left, grad_right = adapter_gradients(low, own, oth)
    low, grad_left, grad_right = lax.optimization_barrier((low, grad_left, grad_right))
    own_terms, sent = adapter_terms(low, weights)
    oth_terms = other_core(sent)
    done = [None] * NX
    for k in (1, 3, 2, 0):
        done[k] = finish(k, at_x, rows[k], own_terms, oth_terms, cots[k], frozen_value_weight)
    gradient, done = scatter_gradients(grad_left, grad_right, y, done)
    output, token_gradient = unpack(at_x, done, base)

    next_down_factors, next_down_first, next_down_second = moment_update(
        down_factors, down_first_moment, down_second_moment, gradient[:, :MS].T[None]
    )
    next_up_factors, next_up_first, next_up_second = moment_update(
        up_factors, up_first_moment, up_second_moment, gradient[:, MS:][None]
    )
    return (
        output,
        token_gradient,
        next_down_factors,
        next_up_factors,
        next_down_first,
        next_down_second,
        next_up_first,
        next_up_second,
    )


def solution(mesh):
    fine = Mesh(mesh.devices.reshape(NY, NZ, NC, NX), ("y", "z", "c", "x"))
    dp = ("y", "z", "c")
    rows = P((*dp, "x"), None)
    down = P(dp, "x", None)
    up = P(dp, None, "x")
    return jax.shard_map(
        local,
        mesh=fine,
        in_specs=(rows, rows, rows, P(), P("x", None), down, up, down, down, up, up),
        out_specs=(rows, rows, down, up, down, down, up, up),
        check_vma=False,
    )
```

```python
import jax
import jax.numpy as jnp
from jax import lax
from jax.experimental import pallas as pl
from jax.experimental.pallas import tpu as pltpu
from jax.sharding import Mesh, PartitionSpec as P

ADAPTER_SCALE = 0.25
BETA_ONE = 0.9
BETA_TWO = 0.99
ADAM_STEP = 10.0
ADAM_RATE = 0.02
ADAM_EPS = 1e-08

NY, NZ, NC, NX = 4, 8, 2, 4
ROWS = 256
MODEL = 5120
KV = 1024
RANK = 64
MS = MODEL // NX
KS = KV // NX
WIDE = MS + KS
LEFT = 512
RIGHT = WIDE - LEFT
REST = MS - LEFT
CODE = 128
SENT = MS + CODE
PER = 2
CAP = 8
GROUP_ROWS = NY * CAP
SLOTS = NZ * GROUP_ROWS
COLS = NY * RANK
BF = jnp.bfloat16
F32 = jnp.float32


def exchange(array, axis):
    return lax.all_to_all(array, axis, split_axis=0, concat_axis=0, tiled=True)


def gather(array, axis, count):
    return exchange(jnp.broadcast_to(array[None], (count, *array.shape)), axis)


def total(array):
    return jnp.sum(array.astype(F32), axis=0)


def shift(count, step):
    return [(i, (i + step) % count) for i in range(count)]


def along_y(array, step):
    return lax.ppermute(array, "y", shift(NY, step))


def along_z(array, step):
    return lax.ppermute(array, "z", shift(NZ, step))


def along_x(array, step):
    return lax.ppermute(array, "x", shift(NX, step))


def other_core(array):
    return lax.ppermute(array, "c", shift(NC, 1))


def moment_update(master, first_moment, second_moment, gradient):
    first_new = BETA_ONE * first_moment + (1.0 - BETA_ONE) * gradient
    second_new = BETA_TWO * second_moment + (1.0 - BETA_TWO) * gradient * gradient
    first_hat = first_new / (1.0 - BETA_ONE**ADAM_STEP)
    second_hat = second_new / (1.0 - BETA_TWO**ADAM_STEP)
    updated = master - ADAM_RATE * first_hat / (jnp.sqrt(second_hat) + ADAM_EPS)
    return (updated, first_new, second_new)


def dot(a, b):
    return jnp.dot(a, b, preferred_element_type=F32)


def dot_t(a, b):
    return lax.dot_general(a, b, (((1,), (1,)), ((), ())), preferred_element_type=F32)


def dot_tn(a, b):
    return lax.dot_general(a, b, (((0,), (0,)), ((), ())), preferred_element_type=F32)


def gather_weights(wide):
    return lax.all_gather(wide, ("y", "z"), axis=0).reshape(NY, NZ, RANK, WIDE)


def part(array, at, count):
    return lax.dynamic_index_in_dim(array, at % count, 0, keepdims=False)


def scatter_gradients(left, right, y, done):
    left = exchange(left, "y")
    right = lax.psum_scatter(right, "z", scatter_dimension=0, tiled=False)
    one, three = along_x(done[1], -1), along_x(done[3], -3)
    half = ROWS // 2
    two, rest = along_x(done[2][:half], -2), along_x(done[2][half:], -2)
    left, one, two, three, own = lax.optimization_barrier((left, one, two, three, done[0]))
    left = exchange(total(left).astype(BF), "z")
    right = right.reshape(NY, RANK, RIGHT)
    near = [along_y(part(right, y - k, NY), -k) for k in range(1, NY)]
    right = part(right, y, NY).astype(F32) + near[0] + near[1] + near[2]
    right, rest = lax.optimization_barrier((right, rest))
    done = [own, one, two, rest, three]
    return jnp.concatenate([total(left), right], axis=1), done


def params(megabytes=56):
    return pltpu.CompilerParams(vmem_limit_bytes=megabytes * 1024 * 1024)


def one_hot(code):
    code = code.astype(F32)
    slot = code[:, 0:1] * GROUP_ROWS + code[:, 1:2]
    slots = lax.broadcasted_iota(jnp.int32, (ROWS, NC * SLOTS), 1).astype(F32)
    return jnp.where(slots == slot, 1.0, 0.0).astype(BF)


def spread_kernel(x, r0, r1, r2, r3, c0, c1, c2, c3, own, oth):
    groups = zip((r0, r1, r2, r3), (c0, c1, c2, c3), strict=True)
    for k, (rows, cot) in enumerate(groups):
        source = pl.ds(lax.rem(x[0] + NX - k, NX), 1)
        place = one_hot(rows[:, MS:])
        for columns, part in ((slice(0, MS), rows[:, :MS]), (slice(MS, WIDE), cot[...])):
            placed = dot_tn(place, part).astype(BF)
            shape = (NZ, 1, GROUP_ROWS, placed.shape[1])
            own[:, source, :, columns] = placed[:SLOTS].reshape(shape)
            oth[:, source, :, columns] = placed[SLOTS:].reshape(shape)


def spread(x, rows, cots):
    out = pl.BlockSpec((NZ, NX, GROUP_ROWS, WIDE), lambda i, x: (0, 0, 0, 0))
    return pl.pallas_call(
        spread_kernel,
        grid_spec=pltpu.PrefetchScalarGridSpec(
            num_scalar_prefetch=1,
            grid=(1,),
            in_specs=[pl.BlockSpec((ROWS, SENT), lambda i, x: (0, 0))] * NX
            + [pl.BlockSpec((ROWS, KS), lambda i, x: (0, x[0]))] * NX,
            out_specs=[out, out],
        ),
        out_shape=[jax.ShapeDtypeStruct((NZ, NX, GROUP_ROWS, WIDE), BF)] * 2,
        compiler_params=params(),
        name="spread_rows",
    )(x, *rows, *cots)


def row_mask():
    rows = lax.broadcasted_iota(jnp.int32, (2 * NX * GROUP_ROWS, COLS), 0)
    cols = lax.broadcasted_iota(jnp.int32, (2 * NX * GROUP_ROWS, COLS), 1)
    return lax.rem(rows, GROUP_ROWS) // CAP == cols // RANK


def fold(product, mask):
    kept = jnp.where(mask, product, 0.0)
    half = kept[:, : 2 * RANK] + kept[:, 2 * RANK :]
    return half + pltpu.roll(half, RANK, 1)


def group_rows(own, oth, j):
    shape = (NX * GROUP_ROWS, WIDE)
    return jnp.concatenate([own[j].reshape(shape), oth[j].reshape(shape)], axis=0)


def low_kernel(own, oth, weights, out):
    mask = row_mask()
    lanes = lax.broadcasted_iota(jnp.int32, out.shape[1:], 1)
    for j in range(PER):
        s = group_rows(own, oth, j)
        w = weights[:, j].reshape(COLS, WIDE)
        low = dot_t(s[:, :MS], w[:, :MS])
        grad = dot_t(s[:, MS:], w[:, MS:])
        out[j] = jnp.where(lanes < RANK, fold(low, mask), fold(grad, mask)).astype(BF)


def slot_spec():
    return pl.BlockSpec((PER, NX, GROUP_ROWS, WIDE), lambda g: (g, 0, 0, 0))


def left_spec(width=LEFT):
    return pl.BlockSpec((NY, PER, RANK, width), lambda g: (0, g, 0, 0))


def right_spec():
    return pl.BlockSpec((PER, COLS, RIGHT), lambda g: (g, 0, 0))


def low_spec():
    return pl.BlockSpec((PER, 2 * NX * GROUP_ROWS, 2 * RANK), lambda g: (g, 0, 0))


def low_partial(own, oth, weights):
    return pl.pallas_call(
        low_kernel,
        grid=(NZ // PER,),
        in_specs=[slot_spec(), slot_spec(), left_spec(WIDE)],
        out_specs=low_spec(),
        out_shape=jax.ShapeDtypeStruct((NZ, 2 * NX * GROUP_ROWS, 2 * RANK), BF),
        compiler_params=params(),
        name="low_partial",
    )(own, oth, weights)


def sum_over_x(partial):
    share = NZ // NX
    parts = exchange(partial.reshape(NX, share, *partial.shape[1:]), "x")
    mine = (ADAPTER_SCALE * total(parts)).astype(BF)
    return gather(mine, "x", NX).reshape(partial.shape)


def masked(low, mask):
    both = low.astype(F32)
    turned = pltpu.roll(both, RANK, 1)
    lanes = lax.broadcasted_iota(jnp.int32, both.shape, 1)
    reduced = jnp.where(lanes < RANK, both, turned)
    gradient = jnp.where(lanes < RANK, turned, both)
    reduced = jnp.where(mask, jnp.concatenate([reduced, reduced], axis=1), 0.0).astype(BF)
    gradient = jnp.where(mask, jnp.concatenate([gradient, gradient], axis=1), 0.0).astype(BF)
    return reduced, gradient


def gradient_kernel(low, own, oth, grad_left, grad_right):
    mask = row_mask()
    for j in range(PER):
        s = group_rows(own, oth, j)
        reduced, gradient = masked(low[j], mask)
        near = dot_tn(gradient, s[:, :LEFT]).astype(BF)
        grad_left[:, j] = near.reshape(NY, RANK, LEFT)
        grad_right[j, :, :REST] = dot_tn(gradient, s[:, LEFT:MS]).astype(BF)
        grad_right[j, :, REST:] = dot_tn(reduced, s[:, MS:]).astype(BF)


def adapter_gradients(low, own, oth):
    return pl.pallas_call(
        gradient_kernel,
        grid=(NZ // PER,),
        in_specs=[low_spec(), slot_spec(), slot_spec()],
        out_specs=[left_spec(), right_spec()],
        out_shape=[
            jax.ShapeDtypeStruct((NY, NZ, RANK, LEFT), BF),
            jax.ShapeDtypeStruct((NZ, COLS, RIGHT), BF),
        ],
        compiler_params=params(),
        name="adapter_gradients",
    )(low, own, oth)


def term_kernel(low, weights, own_out, oth_out):
    mask = row_mask()
    shape = (NX, GROUP_ROWS)
    for j in range(PER):
        w = weights[:, j].reshape(COLS, WIDE)
        reduced, gradient = masked(low[j], mask)
        parts = ((slice(0, MS), gradient), (slice(MS, WIDE), reduced))
        for columns, factor in parts:
            terms = dot(factor, w[:, columns]).astype(BF)
            half, width = terms.shape[0] // 2, terms.shape[1]
            own_out[j, :, :, columns] = terms[:half].reshape(*shape, width)
            oth_out[j, :, :, columns] = terms[half:].reshape(*shape, width)


def adapter_terms(low, weights):
    return pl.pallas_call(
        term_kernel,
        grid=(NZ // PER,),
        in_specs=[low_spec(), left_spec(WIDE)],
        out_specs=[slot_spec(), slot_spec()],
        out_shape=[jax.ShapeDtypeStruct((NZ, NX, GROUP_ROWS, WIDE), BF)] * 2,
        compiler_params=params(),
        name="adapter_terms",
    )(low, weights)


def finish_kernel(x, code, own, oth, cot, weight, out):
    terms = jnp.concatenate([own[...].reshape(SLOTS, WIDE), oth[...].reshape(SLOTS, WIDE)], axis=0)
    rows = dot(one_hot(code[...]), terms)
    out[:, :MS] = (rows[:, :MS] + dot_t(cot[...], weight[...])).astype(BF)
    out[:, MS:] = rows[:, MS:].astype(BF)


def finish(k, x, rows, own, oth, cot, weight):
    slots = pl.BlockSpec((NZ, 1, GROUP_ROWS, WIDE), lambda i, x: (0, (x[0] + NX - k) % NX, 0, 0))
    return pl.pallas_call(
        finish_kernel,
        grid_spec=pltpu.PrefetchScalarGridSpec(
            num_scalar_prefetch=1,
            grid=(1,),
            in_specs=[
                pl.BlockSpec((ROWS, CODE), lambda i, x: (0, MS // CODE)),
                slots,
                slots,
                pl.BlockSpec((ROWS, KV), lambda i, x: (0, 0)),
                pl.BlockSpec((MS, KV), lambda i, x: (0, 0)),
            ],
            out_specs=pl.BlockSpec((ROWS, WIDE), lambda i, x: (0, 0)),
        ),
        out_shape=jax.ShapeDtypeStruct((ROWS, WIDE), BF),
        compiler_params=params(),
        name="token_gradient",
    )(x, rows, own, oth, cot, weight)


def pack_kernel(x, t0, t1, t2, t3, code, o0, o1, o2, o3):
    for tok, out in zip((t0, t1, t2, t3), (o0, o1, o2, o3), strict=True):
        out[:, :MS] = tok[...]
        out[:, MS:] = code[...]


def pack(x, tokens, code):
    def columns(k):
        return pl.BlockSpec((ROWS, MS), lambda i, x: (0, (x[0] + k) % NX))

    return pl.pallas_call(
        pack_kernel,
        grid_spec=pltpu.PrefetchScalarGridSpec(
            num_scalar_prefetch=1,
            grid=(1,),
            in_specs=[columns(k) for k in range(NX)]
            + [pl.BlockSpec((ROWS, CODE), lambda i, x: (0, 0))],
            out_specs=[pl.BlockSpec((ROWS, SENT), lambda i, x: (0, 0))] * NX,
        ),
        out_shape=[jax.ShapeDtypeStruct((ROWS, SENT), BF)] * NX,
        compiler_params=params(),
        name="pack_rows",
    )(x, *[tokens] * NX, code)


def unpack_kernel(x, d0, d1, d2, rest, d3, b0, b1, b2, b3, output, gradient):
    half = ROWS // 2
    for k, start, done in ((0, 0, d0), (1, 0, d1), (2, 0, d2), (2, half, rest), (3, 0, d3)):
        at = lax.rem(x[0] + k, NX)
        rows = slice(start, start + done.shape[0])
        wide = pl.ds(pl.multiple_of(at * MS, MS), MS)
        thin = pl.ds(pl.multiple_of(at * KS, KS), KS)
        gradient[rows, wide] = done[:, :MS]
        summed = done[:, MS:].astype(F32)
        for base in (b0, b1, b2, b3):
            summed = summed + base[rows, thin].astype(F32)
        output[rows, thin] = summed.astype(BF)


def unpack(x, done, base):
    def whole(columns, rows=ROWS):
        return pl.BlockSpec((rows, columns), lambda i, x: (0, 0))

    return pl.pallas_call(
        unpack_kernel,
        grid_spec=pltpu.PrefetchScalarGridSpec(
            num_scalar_prefetch=1,
            grid=(1,),
            in_specs=[whole(WIDE, part.shape[0]) for part in done] + [whole(KV)] * NX,
            out_specs=[whole(KV), whole(MODEL)],
        ),
        out_shape=[
            jax.ShapeDtypeStruct((ROWS, KV), BF),
            jax.ShapeDtypeStruct((ROWS, MODEL), BF),
        ],
        compiler_params=params(),
        name="unpack_rows",
    )(x, *done, *base)


def local(
    tokens,
    cotangent,
    tenant,
    adapter_per_slot,
    frozen_value_weight,
    down_factors,
    up_factors,
    down_first_moment,
    down_second_moment,
    up_first_moment,
    up_second_moment,
):
    x, y, z, c = (lax.axis_index(name) for name in ("x", "y", "z", "c"))

    wide = jnp.concatenate([down_factors[0].astype(BF).T, up_factors[0].astype(BF)], axis=1)

    matches = (tenant == adapter_per_slot[None, :]).astype(jnp.int32)
    earlier = jnp.cumsum(matches, axis=0) - matches
    place = jnp.sum(matches * earlier, axis=1)
    owner = jnp.sum(matches * jnp.arange(NY * NZ * NC, dtype=jnp.int32)[None, :], axis=1)
    core = (owner + c) % NC
    high = (core * NZ + owner // NC % NZ)[:, None]
    low = (owner // (NZ * NC) * CAP + place)[:, None]
    code = jnp.concatenate([high, low, jnp.zeros((ROWS, CODE - 2), jnp.int32)], axis=1).astype(BF)

    weights = gather_weights(wide)
    at_x = x.reshape(1)
    rows = pack(at_x, tokens, code)
    rows = [rows[0]] + [along_x(rows[k], k) for k in range(1, NX)]
    cots = [cotangent] + [along_x(cotangent, k) for k in range(1, NX)]
    base = [dot(part[:, :MS], frozen_value_weight).astype(BF) for part in rows]

    own, sent = spread(at_x, rows, cots)
    oth = other_core(sent)
    oth, base = lax.optimization_barrier((oth, base))
    base = [base[0]] + [along_x(base[k], -k) for k in range(1, NX)]
    oth, base[1], base[3] = lax.optimization_barrier((oth, base[1], base[3]))
    low = sum_over_x(low_partial(own, oth, weights))
    low, base[2] = lax.optimization_barrier((low, base[2]))
    grad_left, grad_right = adapter_gradients(low, own, oth)
    low, grad_left, grad_right = lax.optimization_barrier((low, grad_left, grad_right))
    own_terms, sent = adapter_terms(low, weights)
    oth_terms = other_core(sent)
    done = [None] * NX
    for k in (1, 3, 2, 0):
        done[k] = finish(k, at_x, rows[k], own_terms, oth_terms, cots[k], frozen_value_weight)
    gradient, done = scatter_gradients(grad_left, grad_right, y, done)
    output, token_gradient = unpack(at_x, done, base)

    next_down_factors, next_down_first, next_down_second = moment_update(
        down_factors, down_first_moment, down_second_moment, gradient[:, :MS].T[None]
    )
    next_up_factors, next_up_first, next_up_second = moment_update(
        up_factors, up_first_moment, up_second_moment, gradient[:, MS:][None]
    )
    return (
        output,
        token_gradient,
        next_down_factors,
        next_up_factors,
        next_down_first,
        next_down_second,
        next_up_first,
        next_up_second,
    )


def solution(mesh):
    fine = Mesh(mesh.devices.reshape(NY, NZ, NC, NX), ("y", "z", "c", "x"))
    dp = ("y", "z", "c")
    rows = P((*dp, "x"), None)
    down = P(dp, "x", None)
    up = P(dp, None, "x")
    return jax.shard_map(
        local,
        mesh=fine,
        in_specs=(rows, rows, rows, P(), P("x", None), down, up, down, down, up, up),
        out_specs=(rows, rows, down, up, down, down, up, up),
        check_vma=False,
    )
```

```python
import jax
import jax.numpy as jnp
from jax import lax
from jax.experimental import pallas as pl
from jax.experimental.pallas import tpu as pltpu
from jax.sharding import Mesh, PartitionSpec as P

ADAPTER_SCALE = 0.25
BETA_ONE = 0.9
BETA_TWO = 0.99
ADAM_STEP = 10.0
ADAM_RATE = 0.02
ADAM_EPS = 1e-08

NY, NZ, NC, NX = 4, 8, 2, 4
ROWS = 256
MODEL = 5120
KV = 1024
RANK = 64
MS = MODEL // NX
KS = KV // NX
WIDE = MS + KS
LEFT = 512
RIGHT = WIDE - LEFT
REST = MS - LEFT
CODE = 128
SENT = MS + CODE
PER = 2
CAP = 8
GROUP_ROWS = NY * CAP
SLOTS = NZ * GROUP_ROWS
COLS = NY * RANK
BF = jnp.bfloat16
F32 = jnp.float32


def exchange(array, axis):
    return lax.all_to_all(array, axis, split_axis=0, concat_axis=0, tiled=True)


def gather(array, axis, count):
    return exchange(jnp.broadcast_to(array[None], (count, *array.shape)), axis)


def total(array):
    return jnp.sum(array.astype(F32), axis=0)


def shift(count, step):
    return [(i, (i + step) % count) for i in range(count)]


def along_y(array, step):
    return lax.ppermute(array, "y", shift(NY, step))


def along_z(array, step):
    return lax.ppermute(array, "z", shift(NZ, step))


def along_x(array, step):
    return lax.ppermute(array, "x", shift(NX, step))


def other_core(array):
    return lax.ppermute(array, "c", shift(NC, 1))


def moment_update(master, first_moment, second_moment, gradient):
    first_new = BETA_ONE * first_moment + (1.0 - BETA_ONE) * gradient
    second_new = BETA_TWO * second_moment + (1.0 - BETA_TWO) * gradient * gradient
    first_hat = first_new / (1.0 - BETA_ONE**ADAM_STEP)
    second_hat = second_new / (1.0 - BETA_TWO**ADAM_STEP)
    updated = master - ADAM_RATE * first_hat / (jnp.sqrt(second_hat) + ADAM_EPS)
    return (updated, first_new, second_new)


def dot(a, b):
    return jnp.dot(a, b, preferred_element_type=F32)


def dot_t(a, b):
    return lax.dot_general(a, b, (((1,), (1,)), ((), ())), preferred_element_type=F32)


def dot_tn(a, b):
    return lax.dot_general(a, b, (((0,), (0,)), ((), ())), preferred_element_type=F32)


def gather_weights(wide):
    return lax.all_gather(wide, ("y", "z"), axis=0).reshape(NY, NZ, RANK, WIDE)


def part(array, at, count):
    return lax.dynamic_index_in_dim(array, at % count, 0, keepdims=False)


def scatter_gradients(left, right, y, done):
    left = exchange(left, "y")
    right = lax.psum_scatter(right, "z", scatter_dimension=0, tiled=False)
    one, three = along_x(done[1], -1), along_x(done[3], -3)
    half = ROWS // 2
    two, rest = along_x(done[2][:half], -2), along_x(done[2][half:], -2)
    left, one, three, own, _ = lax.optimization_barrier((left, one, three, done[0], done[2]))
    left = exchange(total(left).astype(BF), "z")
    right = right.reshape(NY, RANK, RIGHT)
    near = [along_y(part(right, y - k, NY), -k) for k in range(1, NY)]
    right = part(right, y, NY).astype(F32) + near[0] + near[1] + near[2]
    right, two, rest = lax.optimization_barrier((right, two, rest))
    done = [own, one, two, rest, three]
    return jnp.concatenate([total(left), right], axis=1), done


def params(megabytes=56):
    return pltpu.CompilerParams(vmem_limit_bytes=megabytes * 1024 * 1024)


def one_hot(code):
    code = code.astype(F32)
    slot = code[:, 0:1] * GROUP_ROWS + code[:, 1:2]
    slots = lax.broadcasted_iota(jnp.int32, (ROWS, NC * SLOTS), 1).astype(F32)
    return jnp.where(slots == slot, 1.0, 0.0).astype(BF)


def spread_kernel(x, r0, r1, r2, r3, c0, c1, c2, c3, own, oth):
    groups = zip((r0, r1, r2, r3), (c0, c1, c2, c3), strict=True)
    for k, (rows, cot) in enumerate(groups):
        source = pl.ds(lax.rem(x[0] + NX - k, NX), 1)
        place = one_hot(rows[:, MS:])
        for columns, part in ((slice(0, MS), rows[:, :MS]), (slice(MS, WIDE), cot[...])):
            placed = dot_tn(place, part).astype(BF)
            shape = (NZ, 1, GROUP_ROWS, placed.shape[1])
            own[:, source, :, columns] = placed[:SLOTS].reshape(shape)
            oth[:, source, :, columns] = placed[SLOTS:].reshape(shape)


def spread(x, rows, cots):
    out = pl.BlockSpec((NZ, NX, GROUP_ROWS, WIDE), lambda i, x: (0, 0, 0, 0))
    return pl.pallas_call(
        spread_kernel,
        grid_spec=pltpu.PrefetchScalarGridSpec(
            num_scalar_prefetch=1,
            grid=(1,),
            in_specs=[pl.BlockSpec((ROWS, SENT), lambda i, x: (0, 0))] * NX
            + [pl.BlockSpec((ROWS, KS), lambda i, x: (0, x[0]))] * NX,
            out_specs=[out, out],
        ),
        out_shape=[jax.ShapeDtypeStruct((NZ, NX, GROUP_ROWS, WIDE), BF)] * 2,
        compiler_params=params(),
        name="spread_rows",
    )(x, *rows, *cots)


def row_mask():
    rows = lax.broadcasted_iota(jnp.int32, (2 * NX * GROUP_ROWS, COLS), 0)
    cols = lax.broadcasted_iota(jnp.int32, (2 * NX * GROUP_ROWS, COLS), 1)
    return lax.rem(rows, GROUP_ROWS) // CAP == cols // RANK


def fold(product, mask):
    kept = jnp.where(mask, product, 0.0)
    half = kept[:, : 2 * RANK] + kept[:, 2 * RANK :]
    return half + pltpu.roll(half, RANK, 1)


def group_rows(own, oth, j):
    shape = (NX * GROUP_ROWS, WIDE)
    return jnp.concatenate([own[j].reshape(shape), oth[j].reshape(shape)], axis=0)


def low_kernel(own, oth, weights, out):
    mask = row_mask()
    lanes = lax.broadcasted_iota(jnp.int32, out.shape[1:], 1)
    for j in range(PER):
        s = group_rows(own, oth, j)
        w = weights[:, j].reshape(COLS, WIDE)
        low = dot_t(s[:, :MS], w[:, :MS])
        grad = dot_t(s[:, MS:], w[:, MS:])
        out[j] = jnp.where(lanes < RANK, fold(low, mask), fold(grad, mask)).astype(BF)


def slot_spec():
    return pl.BlockSpec((PER, NX, GROUP_ROWS, WIDE), lambda g: (g, 0, 0, 0))


def left_spec(width=LEFT):
    return pl.BlockSpec((NY, PER, RANK, width), lambda g: (0, g, 0, 0))


def right_spec():
    return pl.BlockSpec((PER, COLS, RIGHT), lambda g: (g, 0, 0))


def low_spec():
    return pl.BlockSpec((PER, 2 * NX * GROUP_ROWS, 2 * RANK), lambda g: (g, 0, 0))


def low_partial(own, oth, weights):
    return pl.pallas_call(
        low_kernel,
        grid=(NZ // PER,),
        in_specs=[slot_spec(), slot_spec(), left_spec(WIDE)],
        out_specs=low_spec(),
        out_shape=jax.ShapeDtypeStruct((NZ, 2 * NX * GROUP_ROWS, 2 * RANK), BF),
        compiler_params=params(),
        name="low_partial",
    )(own, oth, weights)


def sum_over_x(partial):
    share = NZ // NX
    parts = exchange(partial.reshape(NX, share, *partial.shape[1:]), "x")
    mine = (ADAPTER_SCALE * total(parts)).astype(BF)
    return gather(mine, "x", NX).reshape(partial.shape)


def masked(low, mask):
    both = low.astype(F32)
    turned = pltpu.roll(both, RANK, 1)
    lanes = lax.broadcasted_iota(jnp.int32, both.shape, 1)
    reduced = jnp.where(lanes < RANK, both, turned)
    gradient = jnp.where(lanes < RANK, turned, both)
    reduced = jnp.where(mask, jnp.concatenate([reduced, reduced], axis=1), 0.0).astype(BF)
    gradient = jnp.where(mask, jnp.concatenate([gradient, gradient], axis=1), 0.0).astype(BF)
    return reduced, gradient


def gradient_kernel(low, own, oth, grad_left, grad_right):
    mask = row_mask()
    for j in range(PER):
        s = group_rows(own, oth, j)
        reduced, gradient = masked(low[j], mask)
        near = dot_tn(gradient, s[:, :LEFT]).astype(BF)
        grad_left[:, j] = near.reshape(NY, RANK, LEFT)
        grad_right[j, :, :REST] = dot_tn(gradient, s[:, LEFT:MS]).astype(BF)
        grad_right[j, :, REST:] = dot_tn(reduced, s[:, MS:]).astype(BF)


def adapter_gradients(low, own, oth):
    return pl.pallas_call(
        gradient_kernel,
        grid=(NZ // PER,),
        in_specs=[low_spec(), slot_spec(), slot_spec()],
        out_specs=[left_spec(), right_spec()],
        out_shape=[
            jax.ShapeDtypeStruct((NY, NZ, RANK, LEFT), BF),
            jax.ShapeDtypeStruct((NZ, COLS, RIGHT), BF),
        ],
        compiler_params=params(),
        name="adapter_gradients",
    )(low, own, oth)


def term_kernel(low, weights, own_out, oth_out):
    mask = row_mask()
    shape = (NX, GROUP_ROWS)
    for j in range(PER):
        w = weights[:, j].reshape(COLS, WIDE)
        reduced, gradient = masked(low[j], mask)
        parts = ((slice(0, MS), gradient), (slice(MS, WIDE), reduced))
        for columns, factor in parts:
            terms = dot(factor, w[:, columns]).astype(BF)
            half, width = terms.shape[0] // 2, terms.shape[1]
            own_out[j, :, :, columns] = terms[:half].reshape(*shape, width)
            oth_out[j, :, :, columns] = terms[half:].reshape(*shape, width)


def adapter_terms(low, weights):
    return pl.pallas_call(
        term_kernel,
        grid=(NZ // PER,),
        in_specs=[low_spec(), left_spec(WIDE)],
        out_specs=[slot_spec(), slot_spec()],
        out_shape=[jax.ShapeDtypeStruct((NZ, NX, GROUP_ROWS, WIDE), BF)] * 2,
        compiler_params=params(),
        name="adapter_terms",
    )(low, weights)


def finish_kernel(x, code, own, oth, cot, weight, out):
    terms = jnp.concatenate([own[...].reshape(SLOTS, WIDE), oth[...].reshape(SLOTS, WIDE)], axis=0)
    rows = dot(one_hot(code[...]), terms)
    out[:, :MS] = (rows[:, :MS] + dot_t(cot[...], weight[...])).astype(BF)
    out[:, MS:] = rows[:, MS:].astype(BF)


def finish(k, x, rows, own, oth, cot, weight):
    slots = pl.BlockSpec((NZ, 1, GROUP_ROWS, WIDE), lambda i, x: (0, (x[0] + NX - k) % NX, 0, 0))
    return pl.pallas_call(
        finish_kernel,
        grid_spec=pltpu.PrefetchScalarGridSpec(
            num_scalar_prefetch=1,
            grid=(1,),
            in_specs=[
                pl.BlockSpec((ROWS, CODE), lambda i, x: (0, MS // CODE)),
                slots,
                slots,
                pl.BlockSpec((ROWS, KV), lambda i, x: (0, 0)),
                pl.BlockSpec((MS, KV), lambda i, x: (0, 0)),
            ],
            out_specs=pl.BlockSpec((ROWS, WIDE), lambda i, x: (0, 0)),
        ),
        out_shape=jax.ShapeDtypeStruct((ROWS, WIDE), BF),
        compiler_params=params(),
        name="token_gradient",
    )(x, rows, own, oth, cot, weight)


def pack_kernel(x, t0, t1, t2, t3, code, o0, o1, o2, o3):
    for tok, out in zip((t0, t1, t2, t3), (o0, o1, o2, o3), strict=True):
        out[:, :MS] = tok[...]
        out[:, MS:] = code[...]


def pack(x, tokens, code):
    def columns(k):
        return pl.BlockSpec((ROWS, MS), lambda i, x: (0, (x[0] + k) % NX))

    return pl.pallas_call(
        pack_kernel,
        grid_spec=pltpu.PrefetchScalarGridSpec(
            num_scalar_prefetch=1,
            grid=(1,),
            in_specs=[columns(k) for k in range(NX)]
            + [pl.BlockSpec((ROWS, CODE), lambda i, x: (0, 0))],
            out_specs=[pl.BlockSpec((ROWS, SENT), lambda i, x: (0, 0))] * NX,
        ),
        out_shape=[jax.ShapeDtypeStruct((ROWS, SENT), BF)] * NX,
        compiler_params=params(),
        name="pack_rows",
    )(x, *[tokens] * NX, code)


def unpack_kernel(x, d0, d1, d2, rest, d3, b0, b1, b2, b3, output, gradient):
    half = ROWS // 2
    for k, start, done in ((0, 0, d0), (1, 0, d1), (2, 0, d2), (2, half, rest), (3, 0, d3)):
        at = lax.rem(x[0] + k, NX)
        rows = slice(start, start + done.shape[0])
        wide = pl.ds(pl.multiple_of(at * MS, MS), MS)
        thin = pl.ds(pl.multiple_of(at * KS, KS), KS)
        gradient[rows, wide] = done[:, :MS]
        summed = done[:, MS:].astype(F32)
        for base in (b0, b1, b2, b3):
            summed = summed + base[rows, thin].astype(F32)
        output[rows, thin] = summed.astype(BF)


def unpack(x, done, base):
    def whole(columns, rows=ROWS):
        return pl.BlockSpec((rows, columns), lambda i, x: (0, 0))

    return pl.pallas_call(
        unpack_kernel,
        grid_spec=pltpu.PrefetchScalarGridSpec(
            num_scalar_prefetch=1,
            grid=(1,),
            in_specs=[whole(WIDE, part.shape[0]) for part in done] + [whole(KV)] * NX,
            out_specs=[whole(KV), whole(MODEL)],
        ),
        out_shape=[
            jax.ShapeDtypeStruct((ROWS, KV), BF),
            jax.ShapeDtypeStruct((ROWS, MODEL), BF),
        ],
        compiler_params=params(),
        name="unpack_rows",
    )(x, *done, *base)


def local(
    tokens,
    cotangent,
    tenant,
    adapter_per_slot,
    frozen_value_weight,
    down_factors,
    up_factors,
    down_first_moment,
    down_second_moment,
    up_first_moment,
    up_second_moment,
):
    x, y, z, c = (lax.axis_index(name) for name in ("x", "y", "z", "c"))

    wide = jnp.concatenate([down_factors[0].astype(BF).T, up_factors[0].astype(BF)], axis=1)

    matches = (tenant == adapter_per_slot[None, :]).astype(jnp.int32)
    earlier = jnp.cumsum(matches, axis=0) - matches
    place = jnp.sum(matches * earlier, axis=1)
    owner = jnp.sum(matches * jnp.arange(NY * NZ * NC, dtype=jnp.int32)[None, :], axis=1)
    core = (owner + c) % NC
    high = (core * NZ + owner // NC % NZ)[:, None]
    low = (owner // (NZ * NC) * CAP + place)[:, None]
    code = jnp.concatenate([high, low, jnp.zeros((ROWS, CODE - 2), jnp.int32)], axis=1).astype(BF)

    weights = gather_weights(wide)
    at_x = x.reshape(1)
    rows = pack(at_x, tokens, code)
    rows = [rows[0]] + [along_x(rows[k], k) for k in range(1, NX)]
    cots = [cotangent] + [along_x(cotangent, k) for k in range(1, NX)]
    base = [dot(part[:, :MS], frozen_value_weight).astype(BF) for part in rows]

    own, sent = spread(at_x, rows, cots)
    oth = other_core(sent)
    oth, base = lax.optimization_barrier((oth, base))
    base = [base[0]] + [along_x(base[k], -k) for k in range(1, NX)]
    oth, base[1], base[3] = lax.optimization_barrier((oth, base[1], base[3]))
    low = sum_over_x(low_partial(own, oth, weights))
    low, base[2] = lax.optimization_barrier((low, base[2]))
    grad_left, grad_right = adapter_gradients(low, own, oth)
    low, grad_left, grad_right = lax.optimization_barrier((low, grad_left, grad_right))
    own_terms, sent = adapter_terms(low, weights)
    oth_terms = other_core(sent)
    done = [None] * NX
    for k in (1, 3, 2, 0):
        done[k] = finish(k, at_x, rows[k], own_terms, oth_terms, cots[k], frozen_value_weight)
    gradient, done = scatter_gradients(grad_left, grad_right, y, done)
    output, token_gradient = unpack(at_x, done, base)

    next_down_factors, next_down_first, next_down_second = moment_update(
        down_factors, down_first_moment, down_second_moment, gradient[:, :MS].T[None]
    )
    next_up_factors, next_up_first, next_up_second = moment_update(
        up_factors, up_first_moment, up_second_moment, gradient[:, MS:][None]
    )
    return (
        output,
        token_gradient,
        next_down_factors,
        next_up_factors,
        next_down_first,
        next_down_second,
        next_up_first,
        next_up_second,
    )


def solution(mesh):
    fine = Mesh(mesh.devices.reshape(NY, NZ, NC, NX), ("y", "z", "c", "x"))
    dp = ("y", "z", "c")
    rows = P((*dp, "x"), None)
    down = P(dp, "x", None)
    up = P(dp, None, "x")
    return jax.shard_map(
        local,
        mesh=fine,
        in_specs=(rows, rows, rows, P(), P("x", None), down, up, down, down, up, up),
        out_specs=(rows, rows, down, up, down, down, up, up),
        check_vma=False,
    )
```
